512 devices in a mesh: row: 16 (over z, x_hi), col: 32 (over y, x_lo, core).
Axes of the slice: x: 4 (x_hi: 2, x_lo: 2; x = x_hi * 2 + x_lo), y: 8, z: 8, core: 2. Of those that a mesh axis runs over, the one named last changes fastest.
Arguments:
- alignment: bfloat16 [256, 256, 256], P('col', 'row'), may hold values from -6 to 6
- pair_features: bfloat16 [256, 256, 128], P('row', 'col'), may hold values from -6 to 6
- query_matrix: bfloat16 [256, 256], replicated, may hold values from -0.375 to 0.375
- key_matrix: bfloat16 [256, 256], replicated, may hold values from -0.375 to 0.375
- value_matrix: bfloat16 [256, 256], replicated, may hold values from -0.375 to 0.375
- gate_matrix: bfloat16 [256, 256], replicated, may hold values from -0.375 to 0.375
- output_matrix: bfloat16 [256, 256], replicated, may hold values from -0.375 to 0.375
- bias_weight: bfloat16 [128, 8], replicated, may hold values from -29 to 29
- left_factor_weight: bfloat16 [256, 32], replicated, may hold values from -0.375 to 0.375
- right_factor_weight: bfloat16 [256, 32], replicated, may hold values from -0.375 to 0.375
- outer_weight: bfloat16 [1024, 128], replicated, may hold values from -3 to 3
- outgoing_project: bfloat16 [128, 512], replicated, may hold values from -0.5 to 0.5
- outgoing_gate: bfloat16 [128, 128], replicated, may hold values from -0.5 to 0.5
- outgoing_output: bfloat16 [128, 128], replicated, may hold values from -0.5 to 0.5
- incoming_project: bfloat16 [128, 512], replicated, may hold values from -0.5 to 0.5
- incoming_gate: bfloat16 [128, 128], replicated, may hold values from -0.5 to 0.5
- incoming_output: bfloat16 [128, 128], replicated, may hold values from -0.5 to 0.5
Outputs:
- new_alignment: bfloat16 [256, 256, 256], P('col', 'row')
- new_pair: bfloat16 [256, 256, 128], P('row', 'col')
The draws below stay inside these ranges and needn't reach their ends.
All inputs are finite; a program needn't handle non-finite values.
Results may differ from the reference program's by a relative error of at most 0.022.
Values may be sent and summed in bfloat16 or wider, within the bound.
No kernel may reach another device: no remote copies, remote signals or barrier semaphores. Data moves between devices by JAX's collectives and lax.ppermute only.
A program may use at most 64 MiB of HBM per device.

```python
import math
import jax
import jax.numpy as jnp
from jax import lax

RES_DEV = 16
ALIGN_CHANNELS = 256
PAIR_DIM = 128
HEADS = 8
HEAD_DIM = 32
FACTOR_CHANNELS = 32
TRI_DIM = 128
SEQUENCE_COUNT = 256
RESIDUE_COUNT = 256


def draw_bias_weight(key, part):
    key = jax.random.fold_in(key, 11)
    base = jnp.clip(jax.random.normal(jax.random.fold_in(key, 1), (PAIR_DIM, HEADS), jnp.float32), -4.0, 4.0) / math.sqrt(PAIR_DIM)
    strength = jnp.exp(jax.random.uniform(jax.random.fold_in(key, 2), (HEADS,), jnp.float32, 0.0, math.log(4.0)))
    return (base * strength[None, :]).astype(jnp.bfloat16)


def block_levels(own_key, shape, shards, smallest, top_value):
    def one(position, parts):
        heights = jax.random.uniform(jax.random.fold_in(jax.random.fold_in(own_key, 6), position), (parts,), jnp.float32, smallest / len(shards), top_value / len(shards))
        return jnp.repeat(jnp.exp(heights), shape[position] // parts).reshape((-1,) + (1,) * (len(shape) - position - 1))

    loudness = one(*shards[0])
    for cut in shards[1:]:
        loudness = loudness * one(*cut)
    return loudness


def normal_values(rng, extent, deviation, reach, shards=(), dtype=jnp.bfloat16):
    drawn = jax.random.normal(rng, extent, jnp.float32) * deviation
    if len(shards) > 0:
        drawn = block_levels(rng, extent, shards, -0.22, 0.18) * drawn
    return jnp.clip(drawn, min=-reach, max=reach).astype(dtype)


def setup_inputs(seed: int = 0) -> dict:
    seeds = jax.random.split(jax.random.key(seed), 18)
    alignment = normal_values(seeds[0], (SEQUENCE_COUNT, RESIDUE_COUNT, ALIGN_CHANNELS), 1.0, 6.0, ((0, 32), (1, 16)))
    pair_features = normal_values(seeds[1], (RESIDUE_COUNT, RESIDUE_COUNT, PAIR_DIM), 1.0, 6.0, ((0, 16), (1, 32)))
    query_matrix = normal_values(seeds[2], (ALIGN_CHANNELS, ALIGN_CHANNELS), ALIGN_CHANNELS ** -0.5, 0.375)
    key_matrix = normal_values(seeds[3], (ALIGN_CHANNELS, ALIGN_CHANNELS), ALIGN_CHANNELS ** -0.5, 0.375)
    value_matrix = normal_values(seeds[4], (ALIGN_CHANNELS, ALIGN_CHANNELS), ALIGN_CHANNELS ** -0.5, 0.375)
    gate_matrix = normal_values(seeds[5], (ALIGN_CHANNELS, ALIGN_CHANNELS), ALIGN_CHANNELS ** -0.5, 0.375)
    output_matrix = normal_values(seeds[6], (ALIGN_CHANNELS, ALIGN_CHANNELS), ALIGN_CHANNELS ** -0.5, 0.375)
    bias_weight = draw_bias_weight(jax.random.fold_in(seeds[17], 71), 0)
    left_factor_weight = normal_values(seeds[8], (ALIGN_CHANNELS, FACTOR_CHANNELS), ALIGN_CHANNELS ** -0.5, 0.375)
    right_factor_weight = normal_values(seeds[9], (ALIGN_CHANNELS, FACTOR_CHANNELS), ALIGN_CHANNELS ** -0.5, 0.375)
    outer_weight = normal_values(seeds[10], (FACTOR_CHANNELS * FACTOR_CHANNELS, PAIR_DIM), 0.5, 3.0)
    outgoing_project = normal_values(seeds[11], (PAIR_DIM, 4 * TRI_DIM), PAIR_DIM ** -0.5, 0.5)
    outgoing_gate = normal_values(seeds[12], (PAIR_DIM, PAIR_DIM), PAIR_DIM ** -0.5, 0.5)
    outgoing_output = normal_values(seeds[13], (TRI_DIM, PAIR_DIM), TRI_DIM ** -0.5, 0.5)
    incoming_project = normal_values(seeds[14], (PAIR_DIM, 4 * TRI_DIM), PAIR_DIM ** -0.5, 0.5)
    incoming_gate = normal_values(seeds[15], (PAIR_DIM, PAIR_DIM), PAIR_DIM ** -0.5, 0.5)
    incoming_output = normal_values(seeds[16], (TRI_DIM, PAIR_DIM), TRI_DIM ** -0.5, 0.5)
    return {"alignment": alignment, "pair_features": pair_features, "query_matrix": query_matrix, "key_matrix": key_matrix, "value_matrix": value_matrix, "gate_matrix": gate_matrix, "output_matrix": output_matrix, "bias_weight": bias_weight, "left_factor_weight": left_factor_weight, "right_factor_weight": right_factor_weight, "outer_weight": outer_weight, "outgoing_project": outgoing_project, "outgoing_gate": outgoing_gate, "outgoing_output": outgoing_output, "incoming_project": incoming_project, "incoming_gate": incoming_gate, "incoming_output": incoming_output}


def layer_norm(values):
    values = values.astype(jnp.float32)
    center = values - lax.optimization_barrier(jnp.mean(values, axis=-1, keepdims=True))
    variance = lax.optimization_barrier(jnp.mean(center * center, axis=-1, keepdims=True))
    return center * lax.rsqrt(variance + 1e-05)

def project(values, weight):
    return jnp.dot(values, weight, preferred_element_type=jnp.float32)

def row_attention(alignment, pair_features, query_matrix, key_matrix, value_matrix, gate_matrix, output_matrix, bias_weight):
    normed = layer_norm(alignment).astype(jnp.bfloat16)
    queries = project(normed, query_matrix).astype(jnp.bfloat16).reshape(SEQUENCE_COUNT, RESIDUE_COUNT, HEADS, HEAD_DIM)
    keys = project(normed, key_matrix).astype(jnp.bfloat16).reshape(SEQUENCE_COUNT, RESIDUE_COUNT, HEADS, HEAD_DIM)
    values = project(normed, value_matrix).astype(jnp.bfloat16).reshape(SEQUENCE_COUNT, RESIDUE_COUNT, HEADS, HEAD_DIM)
    gates = jax.nn.sigmoid(project(normed, gate_matrix))
    pair_normed = layer_norm(pair_features).astype(jnp.bfloat16)
    bias_low = jnp.einsum('ijc,ch->hij', pair_normed.astype(jnp.float32), bias_weight.astype(jnp.float32)).astype(jnp.bfloat16)
    bias = lax.optimization_barrier(bias_low).astype(jnp.float32)
    scale = HEAD_DIM ** (-0.5)

    def one_sequence(items):
        query_rows, key_rows, value_rows = items
        scores = jnp.einsum('ihd,jhd->hij', query_rows.astype(jnp.float32), key_rows.astype(jnp.float32)) * scale + bias
        weights = jax.nn.softmax(scores, axis=-1).astype(jnp.bfloat16)
        attended = jnp.einsum('hij,jhd->ihd', weights.astype(jnp.float32), value_rows.astype(jnp.float32))
        return attended.reshape(RESIDUE_COUNT, HEADS * HEAD_DIM)
    attended = lax.map(one_sequence, (queries, keys, values))
    gated = (gates * attended).astype(jnp.bfloat16)
    return (alignment.astype(jnp.float32) + project(gated, output_matrix)).astype(jnp.bfloat16)

def outer_mean(new_alignment, pair_features, left_factor_weight, right_factor_weight, outer_weight):
    normed = layer_norm(new_alignment).astype(jnp.bfloat16)
    left = project(normed, left_factor_weight).astype(jnp.bfloat16)
    right = project(normed, right_factor_weight).astype(jnp.bfloat16)
    blocks = RESIDUE_COUNT // RES_DEV
    left_blocks = left.reshape(SEQUENCE_COUNT, blocks, RES_DEV, FACTOR_CHANNELS).transpose(1, 0, 2, 3).reshape(blocks, SEQUENCE_COUNT, RES_DEV * FACTOR_CHANNELS)
    right_flat = right.reshape(SEQUENCE_COUNT, RESIDUE_COUNT * FACTOR_CHANNELS)

    def one_block(left_block):
        products = jnp.dot(left_block.T, right_flat, preferred_element_type=jnp.float32) * (1.0 / SEQUENCE_COUNT)
        outer = products.reshape(RES_DEV, FACTOR_CHANNELS, RESIDUE_COUNT, FACTOR_CHANNELS).transpose(0, 2, 1, 3)
        outer = outer.reshape(RES_DEV, RESIDUE_COUNT, FACTOR_CHANNELS * FACTOR_CHANNELS).astype(jnp.bfloat16)
        return project(outer, outer_weight)
    update = lax.map(one_block, left_blocks).reshape(RESIDUE_COUNT, RESIDUE_COUNT, PAIR_DIM)
    return (pair_features.astype(jnp.float32) + update).astype(jnp.bfloat16)

def triangle(pair_x, in_weight, gate_x, out_weight, outgoing):
    normed = layer_norm(pair_x).astype(jnp.bfloat16)
    proj = project(normed, in_weight)
    left = (jax.nn.sigmoid(proj[..., :TRI_DIM]) * proj[..., TRI_DIM:2 * TRI_DIM]).astype(jnp.bfloat16)
    right = (jax.nn.sigmoid(proj[..., 2 * TRI_DIM:3 * TRI_DIM]) * proj[..., 3 * TRI_DIM:]).astype(jnp.bfloat16)
    gate = jax.nn.sigmoid(project(normed, gate_x))
    left_cf = jnp.transpose(left, (2, 0, 1)).astype(jnp.float32)
    right_cf = jnp.transpose(right, (2, 0, 1)).astype(jnp.float32)
    if outgoing:
        combined = jnp.einsum('cik,cjk->cij', left_cf, right_cf)
    else:
        combined = jnp.einsum('cki,ckj->cij', left_cf, right_cf)
    combined_norm = layer_norm(jnp.transpose(combined, (1, 2, 0))).astype(jnp.bfloat16)
    return (pair_x.astype(jnp.float32) + gate * project(combined_norm, out_weight)).astype(jnp.bfloat16)

def reference(alignment, pair_features, query_matrix, key_matrix, value_matrix, gate_matrix, output_matrix, bias_weight, left_factor_weight, right_factor_weight, outer_weight, outgoing_project, outgoing_gate, outgoing_output, incoming_project, incoming_gate, incoming_output):
    new_alignment = row_attention(alignment, pair_features, query_matrix, key_matrix, value_matrix, gate_matrix, output_matrix, bias_weight)
    pair_one = outer_mean(new_alignment, pair_features, left_factor_weight, right_factor_weight, outer_weight)
    pair_two = triangle(pair_one, outgoing_project, outgoing_gate, outgoing_output, True)
    new_pair = triangle(pair_two, incoming_project, incoming_gate, incoming_output, False)
    return (new_alignment, new_pair)
```

```python
import jax
import jax.numpy as jnp
from jax import lax
from jax.experimental import pallas as pl
from jax.experimental.pallas import tpu as pltpu
from jax.sharding import PartitionSpec as P

F32 = jnp.float32
BF16 = jnp.bfloat16
ROWS, COLS, CHIPS = 16, 32, 16
SAME_CORE = [[2 * chip + core for chip in range(CHIPS)] for core in range(2)]
SWAP = [(c, c ^ 1) for c in range(COLS)]
TURN = [
    (r * COLS + c, (c // 2) * COLS + 2 * r + c % 2) for r in range(ROWS) for c in range(COLS)
]


def layer_norm(values):
    values = values.astype(F32)
    center = values - jnp.mean(values, axis=-1, keepdims=True)
    variance = jnp.mean(center * center, axis=-1, keepdims=True)
    return center * lax.rsqrt(variance + 1e-05)


def project(values, weight):
    return jnp.dot(values, weight, preferred_element_type=F32)


def exchange(chunks, axis, groups=None):
    return lax.all_to_all(chunks, axis, 0, 0, axis_index_groups=groups)


def spread(block, axis, count, groups=None):
    return exchange(jnp.broadcast_to(block[None], (count,) + block.shape), axis, groups)


def edges(pair_x, in_weight, gate_x):
    normed = layer_norm(pair_x).astype(BF16)
    proj = project(normed, in_weight)
    width = in_weight.shape[1] // 4
    left = (jax.nn.sigmoid(proj[..., :width]) * proj[..., width : 2 * width]).astype(BF16)
    right = (jax.nn.sigmoid(proj[..., 2 * width : 3 * width]) * proj[..., 3 * width :]).astype(BF16)
    gate = jax.nn.sigmoid(project(normed, gate_x))
    return left, right, gate


def finish(pair_x, combined, gate, out_weight):
    combined_norm = layer_norm(combined).astype(BF16)
    return (pair_x.astype(F32) + gate * project(combined_norm, out_weight)).astype(BF16)


def partial_kernel(tile_ref, line_ref, out_ref):
    depth = tile_ref.shape[1]
    lines = line_ref.shape[0]

    def one(g, carry):
        tiles = [tile_ref[g, k].astype(F32) for k in range(depth)]
        for n in range(lines):
            total = tiles[0] * line_ref[n, 0:1, :]
            for k in range(1, depth):
                total = total + tiles[k] * line_ref[n, k : k + 1, :]
            out_ref[g, n] = total.astype(BF16)
        return carry

    lax.fori_loop(0, tile_ref.shape[0], one, 0)


def partial_sums(tiles, lines):
    groups, depth, height, width = tiles.shape
    count = lines.shape[0]
    return pl.pallas_call(
        partial_kernel,
        out_shape=jax.ShapeDtypeStruct((groups, count, height, width), BF16),
        cost_estimate=pl.CostEstimate(
            flops=2 * groups * count * height * width * depth,
            bytes_accessed=2 * groups * height * width * (count + depth),
            transcendentals=0,
        ),
    )(tiles, lines.astype(F32))


def attention(
    alignment, pair_features, query_matrix, key_matrix, value_matrix, gate_matrix, output_matrix, bias_weight
):
    seq_count, row_len, channels = alignment.shape
    heads = bias_weight.shape[1]
    head_dim = channels // heads
    pair_normed = layer_norm(pair_features).astype(BF16)
    bias_local = jnp.einsum(
        "ijc,ch->jhi", pair_normed, bias_weight, preferred_element_type=F32
    ).astype(BF16)
    col_len = bias_local.shape[0]
    bias = spread(bias_local.reshape(col_len, heads * row_len), "col", COLS)
    full_len = COLS * col_len
    bias = bias.reshape(full_len, heads * row_len).T.reshape(heads, row_len, full_len).astype(F32)
    normed = layer_norm(alignment).astype(BF16)
    queries = project(normed, query_matrix).astype(BF16).reshape(seq_count, row_len, heads, head_dim)
    gates = jax.nn.sigmoid(project(normed, gate_matrix))
    both_weights = jnp.concatenate([key_matrix, value_matrix], axis=1)
    everyone = spread(normed, "row", ROWS)
    everyone = jnp.transpose(everyone, (1, 0, 2, 3)).reshape(seq_count, full_len, channels)
    keys_values = project(everyone, both_weights).astype(BF16)
    keys = keys_values[..., :channels].reshape(seq_count, full_len, heads, head_dim)
    values = keys_values[..., channels:].reshape(seq_count, full_len, heads, head_dim)
    scores = (
        jnp.einsum("sihd,sjhd->shij", queries, keys, preferred_element_type=F32) * head_dim ** (-0.5)
        + bias[None]
    )
    highest = jnp.max(scores, axis=-1, keepdims=True)
    expo = jnp.exp(scores - highest)
    weights = (expo / jnp.sum(expo, axis=-1, keepdims=True)).astype(BF16)
    attended = jnp.einsum("shij,sjhd->sihd", weights, values, preferred_element_type=F32)
    gated = (gates * attended.reshape(seq_count, row_len, channels)).astype(BF16)
    return (alignment.astype(F32) + project(gated, output_matrix)).astype(BF16)


def on_device(
    alignment,
    pair_features,
    query_matrix,
    key_matrix,
    value_matrix,
    gate_matrix,
    output_matrix,
    bias_weight,
    left_factor_weight,
    right_factor_weight,
    outer_weight,
    outgoing_project,
    outgoing_gate,
    outgoing_output,
    incoming_project,
    incoming_gate,
    incoming_output,
):
    seq_count, row_len, channels = alignment.shape
    col_len, pair_dim = pair_features.shape[1:]
    core = lax.axis_index("col") % 2
    new_alignment = attention(
        alignment, pair_features, query_matrix, key_matrix, value_matrix, gate_matrix, output_matrix, bias_weight
    )
    outer_dim = left_factor_weight.shape[1]
    outer_normed = layer_norm(new_alignment).astype(BF16)
    right = project(outer_normed, right_factor_weight).astype(BF16)
    left = project(outer_normed, left_factor_weight).astype(BF16)
    width = col_len * outer_dim
    halves = right.reshape(seq_count, 2, width).transpose(1, 0, 2)
    halves = jnp.broadcast_to(halves[None], (CHIPS,) + halves.shape).reshape(COLS, seq_count, width)
    right_half = exchange(halves, "col").reshape(COLS * seq_count, width)
    right_all = lax.ppermute(right_half, ("row", "col"), TURN)
    left_all = spread(left.reshape(seq_count, row_len * outer_dim), "col", COLS)
    total_seqs = COLS * seq_count
    left_all = left_all.reshape(total_seqs, row_len * outer_dim)
    products = jnp.einsum("sa,sb->ab", left_all, right_all, preferred_element_type=F32) * (
        1.0 / total_seqs
    )
    outer = products.reshape(row_len, outer_dim, col_len, outer_dim).transpose(0, 2, 1, 3)
    outer = outer.reshape(row_len, col_len, outer_dim * outer_dim).astype(BF16)
    pair_one = (pair_features.astype(F32) + project(outer, outer_weight)).astype(BF16)

    left_edge, right_edge, gate_one = edges(pair_one, outgoing_project, outgoing_gate)
    right_edge = right_edge.reshape(2, col_len, col_len, pair_dim)
    mine = lax.dynamic_index_in_dim(right_edge, core, 0, keepdims=False)
    theirs = lax.dynamic_index_in_dim(right_edge, 1 - core, 0, keepdims=False)
    swapped = lax.ppermute(jnp.concatenate([left_edge, theirs], axis=0), "col", SWAP)
    lines = jnp.concatenate([left_edge, swapped[:row_len]], axis=1)
    tiles = jnp.concatenate([mine, swapped[row_len:]], axis=1).transpose(1, 0, 2)
    partial = partial_sums(spread(tiles, "row", ROWS), lines)
    partial = exchange(partial, "col", SAME_CORE)
    combined = jnp.sum(partial.astype(F32), axis=0)
    pair_two = finish(pair_one, combined, gate_one, outgoing_output)

    left_edge, right_edge, gate_two = edges(pair_two, incoming_project, incoming_gate)
    lines = right_edge.transpose(1, 0, 2)
    own = spread(left_edge, "col", CHIPS, SAME_CORE)
    other = lax.ppermute(own, "col", SWAP)
    own_sums = partial_sums(own, lines)
    other_sums = partial_sums(other, lines)
    first = jnp.where(core == 0, own_sums, other_sums)
    second = jnp.where(core == 0, other_sums, own_sums)
    partial = exchange(jnp.stack([first, second], axis=1), "row")
    combined_in = jnp.sum(partial.astype(F32), axis=0)
    combined_in = combined_in.transpose(0, 2, 1, 3).reshape(row_len, col_len, pair_dim)
    new_pair = finish(pair_two, combined_in, gate_two, incoming_output)
    return (new_alignment, new_pair)


def solution(mesh):
    rep = (P(),) * 15
    return jax.shard_map(
        on_device,
        mesh=mesh,
        in_specs=(P("col", "row", None), P("row", "col", None)) + rep,
        out_specs=(P("col", "row", None), P("row", "col", None)),
        check_vma=False,
    )
```

```python
import functools

import jax
import jax.numpy as jnp
from jax import lax
from jax.experimental import pallas as pl
from jax.experimental.pallas import tpu as pltpu
from jax.sharding import PartitionSpec as P

F32 = jnp.float32
BF16 = jnp.bfloat16
ROWS, COLS, CHIPS = 16, 32, 16
SAME_CORE = [[2 * chip + core for chip in range(CHIPS)] for core in range(2)]
SWAP = [(c, c ^ 1) for c in range(COLS)]
TURN = [
    (r * COLS + c, (c // 2) * COLS + 2 * r + c % 2) for r in range(ROWS) for c in range(COLS)
]


def layer_norm(values):
    values = values.astype(F32)
    center = values - jnp.mean(values, axis=-1, keepdims=True)
    variance = jnp.mean(center * center, axis=-1, keepdims=True)
    return center * lax.rsqrt(variance + 1e-05)


def sigmoid(values):
    return 1.0 / (1.0 + jnp.exp(-values))


def project(values, weight):
    return jnp.dot(values, weight, preferred_element_type=F32)


def exchange(chunks, axis, groups=None):
    return lax.all_to_all(chunks, axis, 0, 0, axis_index_groups=groups)


def spread(block, axis, count, groups=None):
    return exchange(jnp.broadcast_to(block[None], (count,) + block.shape), axis, groups)


def kernel_call(body, outs, args, scratch=(), flops=0, aliases=None):
    shapes = [jax.ShapeDtypeStruct(s, d) for s, d in outs]
    vmem = pl.BlockSpec(memory_space=pltpu.VMEM)
    size = sum(a.size * a.dtype.itemsize for a in args)
    size += sum(s.size * jnp.dtype(s.dtype).itemsize for s in shapes)
    return pl.pallas_call(
        body,
        out_shape=shapes,
        in_specs=[vmem] * len(args),
        out_specs=[vmem] * len(shapes),
        scratch_shapes=[pltpu.VMEM(s, d) for s, d in scratch],
        input_output_aliases=aliases or {},
        compiler_params=pltpu.CompilerParams(vmem_limit_bytes=40 * 2**20),
        cost_estimate=pl.CostEstimate(flops=flops, bytes_accessed=size, transcendentals=0),
    )(*args)


def double_up(block):
    place = lax.axis_index("col")
    held = block
    for bit in (1, 2, 4, 8, 16):
        met = lax.ppermute(held, "col", [(c, c ^ bit) for c in range(COLS)])
        lower = jnp.where((place & bit) == 0, held, met)
        upper = jnp.where((place & bit) == 0, met, held)
        held = jnp.concatenate([lower, upper], axis=0)
    return held


def normed_kernel(x_ref, chunks_ref):
    normed = layer_norm(x_ref[...]).astype(BF16)
    for member in range(chunks_ref.shape[0]):
        chunks_ref[member] = normed


def start_kernel(x_ref, pair_ref, bias_w_ref, query_w_ref, gate_w_ref, bias_ref, query_ref, gate_ref):
    seqs, rows, channels = x_ref.shape
    height, width, depth = pair_ref.shape
    heads = bias_w_ref.shape[1]
    pair_normed = layer_norm(pair_ref[...].reshape(height * width, depth)).astype(BF16)
    wide = jnp.concatenate(
        [jnp.broadcast_to(bias_w_ref[:, h : h + 1], (depth, rows)) for h in range(heads)], axis=1
    )
    every = project(pair_normed, wide).reshape(height, width, heads * rows)
    lane = lax.broadcasted_iota(jnp.int32, (width, heads * rows), 1) % rows
    bias = jnp.zeros((width, heads * rows), F32)
    for i in range(height):
        bias = jnp.where(lane == i, every[i], bias)
    bias_ref[...] = bias.astype(BF16)
    normed = layer_norm(x_ref[...].reshape(seqs * rows, channels)).astype(BF16)
    query_ref[...] = project(normed, query_w_ref[...]).astype(BF16).reshape(seqs, rows, channels)
    gate_ref[...] = sigmoid(project(normed, gate_w_ref[...]))


def attention_kernel(
    heads, every_ref, bias_ref, query_ref, gate_ref, x_ref, both_w_ref, out_w_ref, factor_w_ref,
    new_ref, left_ref, right_ref, gated_ref, factor_ref,
):
    members, seqs, rows, channels = every_ref.shape
    head_dim = channels // heads
    full = members * rows
    bias = bias_ref[...].astype(F32).T
    head_of = lax.broadcasted_iota(jnp.int32, (rows, channels), 1) // head_dim

    def one(s, carry):
        tokens = every_ref[:, s].reshape(full, channels)
        both = project(tokens, both_w_ref[...]).astype(BF16)
        query = query_ref[s]
        spread_query = jnp.concatenate(
            [jnp.where(head_of == h, query, jnp.zeros_like(query)) for h in range(heads)], axis=0
        )
        scores = lax.dot_general(
            spread_query, both[:, :channels], (((1,), (1,)), ((), ())), preferred_element_type=F32
        )
        scores = scores * head_dim ** (-0.5) + bias
        expo = jnp.exp(scores - jnp.max(scores, axis=-1, keepdims=True))
        weights = (expo / jnp.sum(expo, axis=-1, keepdims=True)).astype(BF16)
        mixed = project(weights, both[:, channels:])
        attended = mixed[0:rows]
        for h in range(1, heads):
            attended = jnp.where(head_of == h, mixed[h * rows : (h + 1) * rows], attended)
        place = pl.ds(pl.multiple_of(s * rows, rows), rows)
        gated_ref[place, :] = (gate_ref[place, :] * attended).astype(BF16)
        return carry

    lax.fori_loop(0, seqs, one, 0, unroll=2)
    tokens = x_ref[...].reshape(seqs * rows, channels).astype(F32)
    new = (tokens + project(gated_ref[...], out_w_ref[...])).astype(BF16)
    new_ref[...] = new.reshape(seqs, rows, channels)
    factor_ref[...] = project(layer_norm(new).astype(BF16), factor_w_ref[...])
    width = left_ref.shape[1] // rows
    pieces = [factor_ref[pl.ds(i, seqs, stride=rows), :] for i in range(rows)]
    left_ref[...] = jnp.concatenate([p[:, :width] for p in pieces], axis=1).astype(BF16)
    right = jnp.concatenate([p[:, width : 2 * width] for p in pieces], axis=1).astype(BF16)
    half = right.shape[1] // 2
    right_ref[0] = right[:, :half]
    right_ref[1] = right[:, half:]


def edge_parts(pair, in_w_ref, gate_w_ref):
    normed = layer_norm(pair).astype(BF16)
    proj = project(normed, in_w_ref[...])
    width = in_w_ref.shape[1] // 4
    left = sigmoid(proj[:, :width]) * proj[:, width : 2 * width]
    right = sigmoid(proj[:, 2 * width : 3 * width]) * proj[:, 3 * width :]
    return left, right, sigmoid(project(normed, gate_w_ref[...]))


def outer_kernel(
    left_ref, right_ref, pair_ref, outer_w_ref, in_w_ref, gate_w_ref,
    pair_out, gate_out, left_out, right_out, products_ref, update_ref, right_scr,
):
    total = left_ref.shape[0]
    rows, cols, depth = pair_ref.shape
    factor = left_ref.shape[1] // rows
    products = lax.dot_general(
        left_ref[...], right_ref[...], (((0,), (0,)), ((), ())), preferred_element_type=F32
    ) * (1.0 / total)
    slabs, _, slab = products_ref.shape
    per_slab = slab // factor
    outer = []
    for part in range(slabs):
        products_ref[part] = products[:, part * slab : (part + 1) * slab]
        lines = [
            products_ref[part, pl.ds(a, rows, stride=factor), :].astype(BF16) for a in range(factor)
        ]
        for j in range(per_slab):
            pieces = [line[:, j * factor : (j + 1) * factor] for line in lines]
            outer.append(jnp.concatenate(pieces, axis=1))
    outer = jnp.concatenate(outer, axis=0)
    update_ref[...] = project(outer, outer_w_ref[...])
    update = jnp.concatenate(
        [update_ref[pl.ds(i, cols, stride=rows), :] for i in range(rows)], axis=0
    )
    pair = (pair_ref[...].reshape(rows * cols, depth).astype(F32) + update).astype(BF16)
    pair_out[...] = pair
    left, right, gate = edge_parts(pair, in_w_ref, gate_w_ref)
    gate_out[...] = gate
    left_out[...] = left.astype(BF16).reshape(rows, cols, depth)
    right_scr[...] = right
    for k in range(cols):
        line = right_scr[pl.ds(k, rows, stride=cols), :].astype(BF16)
        right_out[0, k] = line[:cols]
        right_out[1, k] = line[cols:]


def partial_kernel(axis, tile_ref, *refs):
    line_refs, out_ref, scr = refs[:-2], refs[-2], refs[-1]
    groups, depth = tile_ref.shape[:2]
    lines = out_ref.shape[1]
    start = 0
    for line_ref in line_refs:
        size = line_ref.shape[1]
        scr[:, start : start + size, :] = line_ref[...].astype(F32)
        start += size

    def one(g, carry):
        tiles = [[tile_ref[2 * g + u, k].astype(F32) for k in range(depth)] for u in range(2)]
        for n in range(lines):
            totals = [None, None]
            for k in range(depth):
                line = scr[n, k : k + 1, :]
                for u in range(2):
                    term = tiles[u][k] * line
                    totals[u] = term if k == 0 else totals[u] + term
            for u in range(2):
                out_ref[2 * g + u, n] = totals[u].astype(BF16)
        return carry

    lax.fori_loop(0, groups // 2, one, 0)


def partial_sums(tiles, *lines):
    groups, depth, height, width = tiles.shape
    count = lines[0].shape[0]
    return kernel_call(
        functools.partial(partial_kernel, 0),
        [((groups, count, height, width), BF16)],
        (tiles,) + lines,
        scratch=[((count, depth, width), F32)],
        flops=2 * groups * count * height * width * depth,
    )[0]


def added(partial_ref):
    total = partial_ref[0].astype(F32)
    for member in range(1, partial_ref.shape[0]):
        total = total + partial_ref[member].astype(F32)
    return total


def middle_kernel(
    partial_ref, pair_ref, gate_ref, out_w_ref, in_w_ref, next_gate_w_ref,
    pair_out, gate_out, chunks_out, line_out, right_scr,
):
    rows, cols, depth = partial_ref.shape[1:]
    combined = added(partial_ref).reshape(rows * cols, depth)
    update = project(layer_norm(combined).astype(BF16), out_w_ref[...])
    pair = (pair_ref[...].astype(F32) + gate_ref[...] * update).astype(BF16)
    pair_out[...] = pair
    left, right, gate = edge_parts(pair, in_w_ref, next_gate_w_ref)
    gate_out[...] = gate
    left = left.astype(BF16).reshape(rows, cols, depth)
    for member in range(chunks_out.shape[0]):
        chunks_out[member] = left
    right_scr[...] = right
    for j in range(cols):
        line_out[j] = right_scr[pl.ds(j, rows, stride=cols), :].astype(BF16)


def last_kernel(partial_ref, pair_ref, gate_ref, out_w_ref, new_ref, scr):
    halves, cols, tall, depth = partial_ref.shape[1:]
    scr[...] = added(partial_ref).reshape(halves * cols * tall, depth)
    combined = jnp.concatenate(
        [
            scr[pl.ds(half * cols * tall + i, cols, stride=tall), :]
            for half in range(halves)
            for i in range(tall)
        ],
        axis=0,
    )
    update = project(layer_norm(combined).astype(BF16), out_w_ref[...])
    new = (pair_ref[...].astype(F32) + gate_ref[...] * update).astype(BF16)
    new_ref[...] = new.reshape(new_ref.shape)


def on_device(
    alignment,
    pair_features,
    query_matrix,
    key_matrix,
    value_matrix,
    gate_matrix,
    output_matrix,
    bias_weight,
    left_factor_weight,
    right_factor_weight,
    outer_weight,
    outgoing_project,
    outgoing_gate,
    outgoing_output,
    incoming_project,
    incoming_gate,
    incoming_output,
):
    seqs, rows, channels = alignment.shape
    cols, depth = pair_features.shape[1:]
    heads = bias_weight.shape[1]
    factor = left_factor_weight.shape[1]
    places = rows * cols
    full = COLS * cols
    core = lax.axis_index("col") % 2

    chunks = kernel_call(normed_kernel, [((ROWS, seqs, rows, channels), BF16)], (alignment,))[0]
    everyone = exchange(chunks, "row")
    bias, queries, gates = kernel_call(
        start_kernel,
        [((cols, heads * rows), BF16), ((seqs, rows, channels), BF16), ((seqs * rows, channels), F32)],
        (alignment, pair_features, bias_weight, query_matrix, gate_matrix),
    )
    bias = double_up(bias[None]).reshape(full, heads * rows)
    both_weights = jnp.concatenate([key_matrix, value_matrix], axis=1)
    spare = jnp.zeros((channels, 128 - 2 * factor), BF16)
    factor_weights = jnp.concatenate([left_factor_weight, right_factor_weight, spare], axis=1)
    new_alignment, left, right = kernel_call(
        functools.partial(attention_kernel, heads),
        [
            ((seqs, rows, channels), BF16),
            ((seqs, rows * factor), BF16),
            ((2, seqs, cols * factor), BF16),
        ],
        (everyone, bias, queries, gates, alignment, both_weights, output_matrix, factor_weights),
        scratch=[((seqs * rows, channels), BF16), ((seqs * rows, 128), F32)],
    )

    mine = lax.dynamic_index_in_dim(right, core, 0, keepdims=False)
    theirs = lax.dynamic_index_in_dim(right, 1 - core, 0, keepdims=False)
    swapped = lax.ppermute(theirs, "col", SWAP)
    both = jnp.where(
        core == 0, jnp.concatenate([mine, swapped], axis=0), jnp.concatenate([swapped, mine], axis=0)
    )
    left, both = lax.optimization_barrier((left, both))
    turned = lax.ppermute(both, ("row", "col"), TURN)
    left_all = spread(left, "col", COLS)
    turned, left_all = lax.optimization_barrier((turned, left_all))
    right_all = spread(turned, "row", ROWS).reshape(COLS * seqs, cols * factor)
    left_all = left_all.reshape(COLS * seqs, rows * factor)
    pair_one, gate_one, left_edge, right_edge = kernel_call(
        outer_kernel,
        [
            ((places, depth), BF16),
            ((places, depth), F32),
            ((rows, cols, depth), BF16),
            ((2, cols, cols, depth), BF16),
        ],
        (left_all, right_all, pair_features, outer_weight, outgoing_project, outgoing_gate),
        scratch=[
            ((cols * factor // 128, rows * factor, 128), F32),
            ((places, depth), F32),
            ((places, depth), F32),
        ],
    )

    mine = lax.dynamic_index_in_dim(right_edge, core, 0, keepdims=False)
    theirs = lax.dynamic_index_in_dim(right_edge, 1 - core, 0, keepdims=False)
    swapped = lax.ppermute(jnp.concatenate([left_edge, theirs], axis=0), "col", SWAP)
    tiles = jnp.concatenate([mine, swapped[rows:]], axis=0)
    partial = partial_sums(spread(tiles, "row", ROWS), left_edge, swapped[:rows])
    partial = exchange(partial, "col", SAME_CORE)
    pair_two, gate_two, chunks, lines = kernel_call(
        middle_kernel,
        [
            ((places, depth), BF16),
            ((places, depth), F32),
            ((CHIPS, rows, cols, depth), BF16),
            ((cols, rows, depth), BF16),
        ],
        (partial, pair_one, gate_one, outgoing_output, incoming_project, incoming_gate),
        scratch=[((places, depth), F32)],
    )

    own = exchange(chunks, "col", SAME_CORE)
    other = lax.ppermute(own, "col", SWAP)
    own_sums = partial_sums(own, lines)
    other_sums = partial_sums(other, lines)
    first = jnp.where(core == 0, own_sums, other_sums)
    second = jnp.where(core == 0, other_sums, own_sums)
    partial = exchange(jnp.stack([first, second], axis=1), "row")
    new_pair = kernel_call(
        last_kernel,
        [((rows, cols, depth), BF16)],
        (partial, pair_two, gate_two, incoming_output),
        scratch=[((places, depth), F32)],
    )[0]
    return (new_alignment, new_pair)


def solution(mesh):
    rep = (P(),) * 15
    return jax.shard_map(
        on_device,
        mesh=mesh,
        in_specs=(P("col", "row", None), P("row", "col", None)) + rep,
        out_specs=(P("col", "row", None), P("row", "col", None)),
        check_vma=False,
    )
```

```python
import functools

import jax
import jax.numpy as jnp
from jax import lax
from jax.experimental import pallas as pl
from jax.experimental.pallas import tpu as pltpu
from jax.sharding import PartitionSpec as P

F32 = jnp.float32
BF16 = jnp.bfloat16
ROWS, COLS = 16, 32
SIZES = {"z": 8, "xh": 2, "y": 8, "xl": 2, "core": 2}
ROW, COL = ("z", "xh"), ("y", "xl", "core")
FLIP = [(0, 1), (1, 0)]
CROSS = [(0, 0), (1, 2), (2, 1), (3, 3)]


def layer_norm(values):
    values = values.astype(F32)
    center = values - jnp.mean(values, axis=-1, keepdims=True)
    variance = jnp.mean(center * center, axis=-1, keepdims=True)
    return center * lax.rsqrt(variance + 1e-05)


def sigmoid(values):
    return 1.0 / (1.0 + jnp.exp(-values))


def project(values, weight):
    return jnp.dot(values, weight, preferred_element_type=F32)


def exchange(chunks, axes):
    return lax.all_to_all(chunks, axes, 0, 0)


def flip(block, axis):
    return lax.ppermute(block, axis, FLIP)


def cross(block):
    return lax.ppermute(block, ("xh", "xl"), CROSS)


def in_order(place, own, other, axis=0):
    lower = jnp.where(place == 0, own, other)
    upper = jnp.where(place == 0, other, own)
    return jnp.concatenate([lower, upper], axis=axis)


def kernel_call(body, outs, args, scratch=(), flops=0, aliases=None):
    shapes = [jax.ShapeDtypeStruct(s, d) for s, d in outs]
    vmem = pl.BlockSpec(memory_space=pltpu.VMEM)
    size = sum(a.size * a.dtype.itemsize for a in args)
    size += sum(s.size * jnp.dtype(s.dtype).itemsize for s in shapes)
    return pl.pallas_call(
        body,
        out_shape=shapes,
        in_specs=[vmem] * len(args),
        out_specs=[vmem] * len(shapes),
        scratch_shapes=[pltpu.VMEM(s, d) for s, d in scratch],
        input_output_aliases=aliases or {},
        compiler_params=pltpu.CompilerParams(vmem_limit_bytes=40 * 2**20),
        cost_estimate=pl.CostEstimate(flops=flops, bytes_accessed=size, transcendentals=0),
    )(*args)


def double_up(block, later):
    held = block
    for axis, bit in (("core", 1), ("xl", 1), ("y", 1), ("y", 2), ("y", 4)):
        size = SIZES[axis]
        met = lax.ppermute(held, axis, [(c, c ^ bit) for c in range(size)])
        held = in_order(lax.axis_index(axis) & bit, held, met)
        if axis == "core":
            held, later = lax.optimization_barrier((held, later))
    return held, later


def normed_kernel(x_ref, chunks_ref):
    normed = layer_norm(x_ref[...]).astype(BF16)
    for member in range(chunks_ref.shape[0]):
        chunks_ref[member] = normed


def bias_kernel(rows, pair_ref, bias_w_ref, bias_ref):
    height, width, depth = pair_ref.shape
    heads = bias_w_ref.shape[0]
    pair_normed = layer_norm(pair_ref[...].reshape(height * width, depth)).astype(BF16)
    wide = jnp.concatenate(
        [jnp.broadcast_to(bias_w_ref[h : h + 1, :], (rows, depth)) for h in range(heads)], axis=0
    )
    every = lax.dot_general(
        pair_normed, wide, (((1,), (1,)), ((), ())), preferred_element_type=F32
    ).reshape(height, width, heads * rows)
    lane = lax.broadcasted_iota(jnp.int32, (width, heads * rows), 1) % rows
    bias = jnp.zeros((width, heads * rows), F32)
    for i in range(height):
        bias = jnp.where(lane == i, every[i], bias)
    bias_ref[...] = bias.astype(BF16)


def query_kernel(x_ref, query_w_ref, gate_w_ref, query_ref, gate_ref):
    seqs, rows, channels = x_ref.shape
    normed = layer_norm(x_ref[...].reshape(seqs * rows, channels)).astype(BF16)
    query_ref[...] = project(normed, query_w_ref[...]).astype(BF16).reshape(seqs, rows, channels)
    gate_ref[...] = sigmoid(project(normed, gate_w_ref[...]))


def attention_kernel(
    heads, every_ref, bias_ref, query_ref, gate_ref, x_ref, key_w_ref, value_w_ref, out_w_ref,
    left_w_ref, right_w_ref, new_ref, left_ref, right_ref, gated_ref, factor_ref,
):
    members, seqs, rows, channels = every_ref.shape
    head_dim = channels // heads
    full = members * rows
    bias = bias_ref[...].astype(F32).T
    head_of = lax.broadcasted_iota(jnp.int32, (rows, channels), 1) // head_dim

    def one(s, carry):
        tokens = every_ref[:, s].reshape(full, channels)
        keys = project(tokens, key_w_ref[...]).astype(BF16)
        values = project(tokens, value_w_ref[...]).astype(BF16)
        query = query_ref[s]
        spread_query = jnp.concatenate(
            [jnp.where(head_of == h, query, jnp.zeros_like(query)) for h in range(heads)], axis=0
        )
        scores = lax.dot_general(
            spread_query, keys, (((1,), (1,)), ((), ())), preferred_element_type=F32
        )
        scores = scores * head_dim ** (-0.5) + bias
        expo = jnp.exp(scores - jnp.max(scores, axis=-1, keepdims=True))
        weights = (expo / jnp.sum(expo, axis=-1, keepdims=True)).astype(BF16)
        mixed = project(weights, values)
        attended = mixed[0:rows]
        for h in range(1, heads):
            attended = jnp.where(head_of == h, mixed[h * rows : (h + 1) * rows], attended)
        place = pl.ds(pl.multiple_of(s * rows, rows), rows)
        gated_ref[place, :] = (gate_ref[place, :] * attended).astype(BF16)
        return carry

    lax.fori_loop(0, seqs, one, 0, unroll=2)
    tokens = x_ref[...].reshape(seqs * rows, channels).astype(F32)
    new = (tokens + project(gated_ref[...], out_w_ref[...])).astype(BF16)
    new_ref[...] = new.reshape(seqs, rows, channels)
    width = left_w_ref.shape[0]
    factor_w = jnp.concatenate([left_w_ref[...], right_w_ref[...]], axis=0)
    factor_ref[:, : 2 * width] = lax.dot_general(
        layer_norm(new).astype(BF16), factor_w, (((1,), (1,)), ((), ())), preferred_element_type=F32
    )
    pieces = [factor_ref[pl.ds(i, seqs, stride=rows), :] for i in range(rows)]
    left_ref[...] = jnp.concatenate([p[:, :width] for p in pieces], axis=1).astype(BF16)
    right = jnp.concatenate([p[:, width : 2 * width] for p in pieces], axis=1).astype(BF16)
    for member in range(right_ref.shape[0]):
        right_ref[member] = right


def factor_kernel(left_ref, right_ref, chunks_ref):
    members, _, size = right_ref.shape
    pieces = chunks_ref.shape[0] // members
    split = size // pieces
    left = left_ref[...]
    for place in range(chunks_ref.shape[0]):
        part = place % pieces
        chunks_ref[place, :, : left.shape[1]] = left
        chunks_ref[place, :, left.shape[1] :] = right_ref[
            place // pieces, :, part * split : (part + 1) * split
        ]


def tile_kernel(mine_ref, theirs_ref, chunks_ref):
    own = mine_ref.shape[0]
    for member in range(chunks_ref.shape[0]):
        chunks_ref[member, :own] = mine_ref[...]
        chunks_ref[member, own:] = theirs_ref[...]


def edge_parts(pair, in_w_ref):
    normed = layer_norm(pair).astype(BF16)
    proj = project(normed, in_w_ref[...])
    width = in_w_ref.shape[1] // 4
    left = sigmoid(proj[:, :width]) * proj[:, width : 2 * width]
    right = sigmoid(proj[:, 2 * width : 3 * width]) * proj[:, 3 * width :]
    return left, right


def updated(combined, pair, gate_w_ref, out_w_ref):
    gate = sigmoid(project(layer_norm(pair).astype(BF16), gate_w_ref[...]))
    update = project(layer_norm(combined).astype(BF16), out_w_ref[...])
    return (pair.astype(F32) + gate * update).astype(BF16)


def outer_kernel(
    factors_ref, pair_ref, outer_w_ref, in_w_ref,
    pair_out, left_out, right_out, products_ref, update_ref, right_scr,
):
    total, size = factors_ref.shape
    rows, cols, depth = pair_ref.shape
    factor = size // (rows + cols)
    products = lax.dot_general(
        factors_ref[:, : rows * factor], factors_ref[:, rows * factor :], (((0,), (0,)), ((), ())), preferred_element_type=F32
    ) * (1.0 / total)
    slabs, _, slab = products_ref.shape
    per_slab = slab // factor
    outer = []
    for part in range(slabs):
        products_ref[part] = products[:, part * slab : (part + 1) * slab]
        lines = [
            products_ref[part, pl.ds(a, rows, stride=factor), :].astype(BF16) for a in range(factor)
        ]
        for j in range(per_slab):
            pieces = [line[:, j * factor : (j + 1) * factor] for line in lines]
            outer.append(jnp.concatenate(pieces, axis=1))
    outer = jnp.concatenate(outer, axis=0)
    update_ref[...] = project(outer, outer_w_ref[...])
    update = jnp.concatenate(
        [update_ref[pl.ds(i, cols, stride=rows), :] for i in range(rows)], axis=0
    )
    pair = (pair_ref[...].reshape(rows * cols, depth).astype(F32) + update).astype(BF16)
    pair_out[...] = pair
    left, right = edge_parts(pair, in_w_ref)
    left_out[...] = left.astype(BF16).reshape(rows, cols, depth)
    right_scr[...] = right
    for k in range(cols):
        line = right_scr[pl.ds(k, rows, stride=cols), :].astype(BF16)
        right_out[0, k] = line[:cols]
        right_out[1, k] = line[cols:]


def partial_kernel(tile_ref, line_ref, *refs):
    before_ref, out_ref, scr = refs if len(refs) == 3 else (None,) + refs
    groups, depth = tile_ref.shape[:2]
    lines = line_ref.shape[0]
    scr[...] = line_ref[...].astype(F32)

    def one(g, carry):
        tiles = [[tile_ref[2 * g + u, k].astype(F32) for k in range(depth)] for u in range(2)]
        for n in range(lines):
            totals = [None, None]
            for k in range(depth):
                line = scr[n, k : k + 1, :]
                for u in range(2):
                    term = tiles[u][k] * line
                    totals[u] = term if k == 0 else totals[u] + term
            for u in range(2):
                if before_ref is None:
                    out_ref[2 * g + u, n] = totals[u].astype(BF16)
                else:
                    part, line_place = divmod(n, out_ref.shape[3])
                    out_ref[2 * g + u, part, 0, line_place] = before_ref[2 * g + u, n]
                    out_ref[2 * g + u, part, 1, line_place] = totals[u].astype(BF16)
        return carry

    lax.fori_loop(0, groups // 2, one, 0)


def partial_sums(tiles, lines, before=None):
    groups, depth, height, width = tiles.shape
    count = lines.shape[0]
    shape = (groups, count, height, width)
    if before is not None:
        shape = (groups, 2, 2, count // 2, height, width)
    return kernel_call(
        partial_kernel,
        [(shape, BF16)],
        (tiles, lines) if before is None else (tiles, lines, before),
        scratch=[((count, depth, width), F32)],
        flops=2 * groups * count * height * width * depth,
    )[0]


def added(partial_ref):
    total = partial_ref[0].astype(F32)
    for member in range(1, partial_ref.shape[0]):
        total = total + partial_ref[member].astype(F32)
    return total


def middle_kernel(
    partial_ref, pair_ref, gate_w_ref, out_w_ref, in_w_ref, pair_out, chunks_out, line_out, right_scr
):
    rows, cols, depth = partial_ref.shape[1:]
    combined = added(partial_ref).reshape(rows * cols, depth)
    pair = updated(combined, pair_ref[...], gate_w_ref, out_w_ref)
    pair_out[...] = pair
    left, right = edge_parts(pair, in_w_ref)
    left = left.astype(BF16).reshape(rows, cols, depth)
    for member in range(chunks_out.shape[0]):
        chunks_out[member] = left
    right_scr[...] = right
    for j in range(cols):
        line_out[j] = right_scr[pl.ds(j, rows, stride=cols), :].astype(BF16)


def last_kernel(core_ref, partial_ref, pair_ref, gate_w_ref, out_w_ref, new_ref, scr):
    halves, cols, tall, depth = partial_ref.shape[1:]
    scr[...] = added(partial_ref).reshape(halves * cols * tall, depth)
    own, other = [
        jnp.concatenate(
            [scr[pl.ds(half * cols * tall + i, cols, stride=tall), :] for i in range(tall)], axis=0
        )
        for half in range(halves)
    ]
    first = core_ref[0:1, :] == 0
    combined = jnp.concatenate(
        [jnp.where(first, own, other), jnp.where(first, other, own)], axis=0
    )
    new_ref[...] = updated(combined, pair_ref[...], gate_w_ref, out_w_ref).reshape(new_ref.shape)


def on_device(
    alignment,
    pair_features,
    query_matrix,
    key_matrix,
    value_matrix,
    gate_matrix,
    output_matrix,
    bias_weight,
    left_factor_weight,
    right_factor_weight,
    outer_weight,
    outgoing_project,
    outgoing_gate,
    outgoing_output,
    incoming_project,
    incoming_gate,
    incoming_output,
):
    seqs, rows, channels = alignment.shape
    cols, depth = pair_features.shape[1:]
    heads = bias_weight.shape[1]
    factor = left_factor_weight.shape[1]
    places = rows * cols
    full = COLS * cols
    core, x_hi = lax.axis_index("core"), lax.axis_index("xh")

    bias = kernel_call(
        functools.partial(bias_kernel, rows), [((cols, heads * rows), BF16)], (pair_features, bias_weight.T)
    )[0]
    chunks = kernel_call(normed_kernel, [((ROWS, seqs, rows, channels), BF16)], (alignment,))[0]
    everyone = exchange(chunks, ROW)
    bias, query_matrix = double_up(bias[None], query_matrix)
    queries, gates = kernel_call(
        query_kernel,
        [((seqs, rows, channels), BF16), ((seqs * rows, channels), F32)],
        (alignment, query_matrix, gate_matrix),
    )
    new_alignment, left, right = kernel_call(
        functools.partial(attention_kernel, heads),
        [
            ((seqs, rows, channels), BF16),
            ((seqs, rows * factor), BF16),
            ((ROWS, seqs, rows * factor), BF16),
        ],
        (
            everyone, bias.reshape(full, heads * rows), queries, gates, alignment, key_matrix,
            value_matrix, output_matrix, left_factor_weight.T, right_factor_weight.T,
        ),
        scratch=[((seqs * rows, channels), BF16), ((seqs * rows, 128), F32)],
    )

    size = (rows + cols) * factor
    chunks = kernel_call(
        factor_kernel, [((COLS, seqs, size), BF16)], (left, exchange(right, ROW))
    )[0]
    factors = exchange(chunks, COL).reshape(COLS * seqs, size)
    pair_one, left_edge, right_edge = kernel_call(
        outer_kernel,
        [((places, depth), BF16), ((rows, cols, depth), BF16), ((2, cols, cols, depth), BF16)],
        (factors, pair_features, outer_weight, outgoing_project),
        scratch=[
            ((cols * factor // 128, rows * factor, 128), F32),
            ((places, depth), F32),
            ((places, depth), F32),
        ],
    )

    mine = lax.dynamic_index_in_dim(right_edge, core, 0, keepdims=False)
    theirs = lax.dynamic_index_in_dim(right_edge, 1 - core, 0, keepdims=False)
    swapped = flip(jnp.concatenate([left_edge, theirs], axis=0), "core")
    chunks = kernel_call(
        tile_kernel, [((SIZES["z"], 2 * cols, cols, depth), BF16)], (mine, swapped[rows:])
    )[0]
    tiles = exchange(chunks, "z")
    lines = jnp.concatenate([left_edge, swapped[:rows]], axis=1)
    lines = in_order(x_hi, lines, flip(lines, "xh"))
    partial = partial_sums(tiles, lines).reshape(ROWS, rows, cols, depth)
    partial = exchange(partial, ("y", "xl"))
    pair_two, chunks, lines = kernel_call(
        middle_kernel,
        [
            ((places, depth), BF16),
            ((SIZES["y"], rows, cols, depth), BF16),
            ((cols, rows, depth), BF16),
        ],
        (partial, cross(pair_one), outgoing_gate, outgoing_output, incoming_project),
        scratch=[((places, depth), F32)],
    )

    own = exchange(chunks, "y")
    lines = in_order(x_hi, lines, flip(lines, "xh"))
    other = flip(own, "core")
    partial = partial_sums(other, lines, partial_sums(own, lines))
    partial = exchange(partial.reshape(ROWS, 2, cols, cols, depth), ("z", "xl"))
    new_pair = kernel_call(
        last_kernel,
        [((rows, cols, depth), BF16)],
        (jnp.full((8, depth), core), partial, cross(pair_two), incoming_gate, incoming_output),
        scratch=[((places, depth), F32)],
    )[0]
    return (new_alignment, new_pair)


def solution(mesh):
    fine = jax.sharding.Mesh(mesh.devices.reshape(tuple(SIZES.values())), tuple(SIZES))
    rep = (P(),) * 15
    return jax.shard_map(
        on_device,
        mesh=fine,
        in_specs=(P(COL, ROW, None), P(ROW, COL, None)) + rep,
        out_specs=(P(COL, ROW, None), P(ROW, COL, None)),
        check_vma=False,
    )
```

```python
import functools

import jax
import jax.numpy as jnp
from jax import lax
from jax.experimental import pallas as pl
from jax.experimental.pallas import tpu as pltpu
from jax.sharding import PartitionSpec as P

F32 = jnp.float32
BF16 = jnp.bfloat16
ROWS, COLS = 16, 32
SIZES = {"z": 8, "xh": 2, "y": 8, "xl": 2, "core": 2}
ROW, COL = ("z", "xh"), ("y", "xl", "core")
ROW_X_FIRST, COL_X_FIRST = ("xh", "z"), ("core", "xl", "y")
FLIP = [(0, 1), (1, 0)]
CROSS = [(0, 0), (1, 2), (2, 1), (3, 3)]


def layer_norm(values):
    values = values.astype(F32)
    center = values - jnp.mean(values, axis=-1, keepdims=True)
    variance = jnp.mean(center * center, axis=-1, keepdims=True)
    return center * lax.rsqrt(variance + 1e-05)


def sigmoid(values):
    return 1.0 / (1.0 + jnp.exp(-values))


def project(values, weight):
    return jnp.dot(values, weight, preferred_element_type=F32)


def exchange(chunks, axes):
    return lax.all_to_all(chunks, axes, 0, 0)


def flip(block, axis):
    return lax.ppermute(block, axis, FLIP)


def cross(block):
    return lax.ppermute(block, ("xh", "xl"), CROSS)


def in_order(place, own, other, axis=0):
    lower = jnp.where(place == 0, own, other)
    upper = jnp.where(place == 0, other, own)
    return jnp.concatenate([lower, upper], axis=axis)


def kernel_call(body, outs, args, scratch=(), flops=0, aliases=None):
    shapes = [jax.ShapeDtypeStruct(s, d) for s, d in outs]
    vmem = pl.BlockSpec(memory_space=pltpu.VMEM)
    size = sum(a.size * a.dtype.itemsize for a in args)
    size += sum(s.size * jnp.dtype(s.dtype).itemsize for s in shapes)
    return pl.pallas_call(
        body,
        out_shape=shapes,
        in_specs=[vmem] * len(args),
        out_specs=[vmem] * len(shapes),
        scratch_shapes=[pltpu.VMEM(s, d) for s, d in scratch],
        input_output_aliases=aliases or {},
        compiler_params=pltpu.CompilerParams(vmem_limit_bytes=40 * 2**20),
        cost_estimate=pl.CostEstimate(flops=flops, bytes_accessed=size, transcendentals=0),
    )(*args)


def shifted(block, step):
    size = SIZES["y"]
    return lax.ppermute(block, "y", [(y, (y - step) % size) for y in range(size)])


def from_col(block, later):
    held = block[None, None, None]
    held = in_order(lax.axis_index("core"), held, flip(held, "core"), 2)
    held, later = lax.optimization_barrier((held, later))
    near = jnp.concatenate([shifted(held, -1), held, shifted(held, 1)], axis=1)
    far = jnp.concatenate([shifted(near[:, 1:], -3), near, shifted(near, 3)], axis=1)
    size = SIZES["y"]
    start = lax.rem(size + 3 - lax.axis_index("y"), size)
    held = lax.dynamic_slice_in_dim(jnp.concatenate([far, far], axis=1), start, size, 1)
    return in_order(lax.axis_index("xl"), held, flip(held, "xl"), 0), later


def normed_kernel(x_ref, chunks_ref):
    normed = layer_norm(x_ref[...]).astype(BF16)
    for member in range(chunks_ref.shape[0]):
        chunks_ref[member] = normed


def bias_kernel(rows, pair_ref, bias_w_ref, bias_ref):
    height, width, depth = pair_ref.shape
    heads = bias_w_ref.shape[0]
    pair_normed = layer_norm(pair_ref[...].reshape(height * width, depth)).astype(BF16)
    wide = jnp.concatenate(
        [jnp.broadcast_to(bias_w_ref[h : h + 1, :], (rows, depth)) for h in range(heads)], axis=0
    )
    every = lax.dot_general(
        pair_normed, wide, (((1,), (1,)), ((), ())), preferred_element_type=F32
    ).reshape(height, width, heads * rows)
    lane = lax.broadcasted_iota(jnp.int32, (width, heads * rows), 1) % rows
    bias = jnp.zeros((width, heads * rows), F32)
    for i in range(height):
        bias = jnp.where(lane == i, every[i], bias)
    bias_ref[...] = bias.astype(BF16)


def query_kernel(x_ref, query_w_ref, gate_w_ref, query_ref, gate_ref):
    seqs, rows, channels = x_ref.shape
    normed = layer_norm(x_ref[...].reshape(seqs * rows, channels)).astype(BF16)
    query_ref[...] = project(normed, query_w_ref[...]).astype(BF16).reshape(seqs, rows, channels)
    gate_ref[...] = sigmoid(project(normed, gate_w_ref[...]))


def attention_kernel(
    heads, every_ref, bias_ref, query_ref, gate_ref, x_ref, key_w_ref, value_w_ref, out_w_ref,
    left_w_ref, right_w_ref, new_ref, left_ref, right_ref, gated_ref, factor_ref,
):
    members, seqs, rows, channels = every_ref.shape
    head_dim = channels // heads
    full = members * rows
    bias = bias_ref[...].astype(F32).T
    head_of = lax.broadcasted_iota(jnp.int32, (rows, channels), 1) // head_dim

    def one(s, carry):
        tokens = every_ref[:, s].reshape(full, channels)
        keys = project(tokens, key_w_ref[...]).astype(BF16)
        values = project(tokens, value_w_ref[...]).astype(BF16)
        query = query_ref[s]
        spread_query = jnp.concatenate(
            [jnp.where(head_of == h, query, jnp.zeros_like(query)) for h in range(heads)], axis=0
        )
        scores = lax.dot_general(
            spread_query, keys, (((1,), (1,)), ((), ())), preferred_element_type=F32
        )
        scores = scores * head_dim ** (-0.5) + bias
        expo = jnp.exp(scores - jnp.max(scores, axis=-1, keepdims=True))
        weights = (expo / jnp.sum(expo, axis=-1, keepdims=True)).astype(BF16)
        mixed = project(weights, values)
        attended = mixed[0:rows]
        for h in range(1, heads):
            attended = jnp.where(head_of == h, mixed[h * rows : (h + 1) * rows], attended)
        place = pl.ds(pl.multiple_of(s * rows, rows), rows)
        gated_ref[place, :] = (gate_ref[place, :] * attended).astype(BF16)
        return carry

    lax.fori_loop(0, seqs, one, 0, unroll=True)
    tokens = x_ref[...].reshape(seqs * rows, channels).astype(F32)
    new = (tokens + project(gated_ref[...], out_w_ref[...])).astype(BF16)
    new_ref[...] = new.reshape(seqs, rows, channels)
    width = left_w_ref.shape[0]
    factor_w = jnp.concatenate([left_w_ref[...], right_w_ref[...]], axis=0)
    factor_ref[:, : 2 * width] = lax.dot_general(
        layer_norm(new).astype(BF16), factor_w, (((1,), (1,)), ((), ())), preferred_element_type=F32
    )
    pieces = [factor_ref[pl.ds(i, seqs, stride=rows), :] for i in range(rows)]
    left_ref[...] = jnp.concatenate([p[:, :width] for p in pieces], axis=1).astype(BF16)
    right = jnp.concatenate([p[:, width : 2 * width] for p in pieces], axis=1).astype(BF16)
    for member in range(right_ref.shape[0]):
        right_ref[member] = right


def factor_kernel(left_ref, right_ref, chunks_ref):
    members, _, size = right_ref.shape
    pieces = chunks_ref.shape[0] // members
    split = size // pieces
    left = left_ref[...]
    for place in range(chunks_ref.shape[0]):
        part = place // members
        chunks_ref[place, :, : left.shape[1]] = left
        chunks_ref[place, :, left.shape[1] :] = right_ref[
            place % members, :, part * split : (part + 1) * split
        ]


def tile_kernel(mine_ref, theirs_ref, chunks_ref):
    own = mine_ref.shape[0]
    for member in range(chunks_ref.shape[0]):
        chunks_ref[member, :own] = mine_ref[...]
        chunks_ref[member, own:] = theirs_ref[...]


def edge_parts(pair, in_w_ref):
    normed = layer_norm(pair).astype(BF16)
    proj = project(normed, in_w_ref[...])
    width = in_w_ref.shape[1] // 4
    left = sigmoid(proj[:, :width]) * proj[:, width : 2 * width]
    right = sigmoid(proj[:, 2 * width : 3 * width]) * proj[:, 3 * width :]
    return left, right


def updated(combined, pair, gate_w_ref, out_w_ref):
    gate = sigmoid(project(layer_norm(pair).astype(BF16), gate_w_ref[...]))
    update = project(layer_norm(combined).astype(BF16), out_w_ref[...])
    return (pair.astype(F32) + gate * update).astype(BF16)


def outer_kernel(
    factors_ref, pair_ref, outer_w_ref, in_w_ref,
    pair_out, left_out, right_out, products_ref, update_ref, right_scr,
):
    total, size = factors_ref.shape
    rows, cols, depth = pair_ref.shape
    factor = size // (rows + cols)
    products = lax.dot_general(
        factors_ref[:, : rows * factor], factors_ref[:, rows * factor :], (((0,), (0,)), ((), ())), preferred_element_type=F32
    ) * (1.0 / total)
    slabs, _, slab = products_ref.shape
    per_slab = slab // factor
    outer = []
    for part in range(slabs):
        products_ref[part] = products[:, part * slab : (part + 1) * slab]
        lines = [
            products_ref[part, pl.ds(a, rows, stride=factor), :].astype(BF16) for a in range(factor)
        ]
        for j in range(per_slab):
            pieces = [line[:, j * factor : (j + 1) * factor] for line in lines]
            outer.append(jnp.concatenate(pieces, axis=1))
    outer = jnp.concatenate(outer, axis=0)
    update_ref[...] = project(outer, outer_w_ref[...])
    update = jnp.concatenate(
        [update_ref[pl.ds(i, cols, stride=rows), :] for i in range(rows)], axis=0
    )
    pair = (pair_ref[...].reshape(rows * cols, depth).astype(F32) + update).astype(BF16)
    pair_out[...] = pair
    left, right = edge_parts(pair, in_w_ref)
    left_out[...] = left.astype(BF16).reshape(rows, cols, depth)
    right_scr[...] = right
    for k in range(cols):
        line = right_scr[pl.ds(k, rows, stride=cols), :].astype(BF16)
        right_out[0, k] = line[:cols]
        right_out[1, k] = line[cols:]


def partial_kernel(tile_ref, line_ref, *refs):
    before_ref, out_ref, scr = refs if len(refs) == 3 else (None,) + refs
    groups, depth = tile_ref.shape[:2]
    scr[...] = line_ref[...].astype(F32)
    per_part = out_ref.shape[-3]

    def one(g, carry):
        tiles = [[tile_ref[2 * g + u, k].astype(F32) for k in range(depth)] for u in range(2)]
        for n in range(line_ref.shape[0]):
            part, place = divmod(n, per_part)
            totals = [None, None]
            for k in range(depth):
                line = scr[n, k : k + 1, :]
                for u in range(2):
                    term = tiles[u][k] * line
                    totals[u] = term if k == 0 else totals[u] + term
            for u in range(2):
                if before_ref is None:
                    out_ref[part, 2 * g + u, place] = totals[u].astype(BF16)
                else:
                    out_ref[part, 2 * g + u, 0, place] = before_ref[part, 2 * g + u, place]
                    out_ref[part, 2 * g + u, 1, place] = totals[u].astype(BF16)
        return carry

    lax.fori_loop(0, groups // 2, one, 0)


def partial_sums(tiles, lines, before=None):
    groups, depth, height, width = tiles.shape
    count = lines.shape[0]
    beside = () if before is None else (2,)
    return kernel_call(
        partial_kernel,
        [((2, groups) + beside + (count // 2, height, width), BF16)],
        (tiles, lines) if before is None else (tiles, lines, before),
        scratch=[((count, depth, width), F32)],
        flops=2 * groups * count * height * width * depth,
    )[0]


def added(partial_ref):
    total = partial_ref[0].astype(F32)
    for member in range(1, partial_ref.shape[0]):
        total = total + partial_ref[member].astype(F32)
    return total


def middle_kernel(
    partial_ref, pair_ref, gate_w_ref, out_w_ref, in_w_ref, pair_out, chunks_out, line_out, right_scr
):
    rows, cols, depth = partial_ref.shape[1:]
    combined = added(partial_ref).reshape(rows * cols, depth)
    pair = updated(combined, pair_ref[...], gate_w_ref, out_w_ref)
    pair_out[...] = pair
    left, right = edge_parts(pair, in_w_ref)
    left = left.astype(BF16).reshape(rows, cols, depth)
    for member in range(chunks_out.shape[0]):
        chunks_out[member] = left
    right_scr[...] = right
    for j in range(cols):
        line_out[j] = right_scr[pl.ds(j, rows, stride=cols), :].astype(BF16)


def last_kernel(core_ref, partial_ref, pair_ref, gate_w_ref, out_w_ref, new_ref, scr):
    halves, cols, tall, depth = partial_ref.shape[1:]
    scr[...] = added(partial_ref).reshape(halves * cols * tall, depth)
    own, other = [
        jnp.concatenate(
            [scr[pl.ds(half * cols * tall + i, cols, stride=tall), :] for i in range(tall)], axis=0
        )
        for half in range(halves)
    ]
    first = core_ref[0:1, :] == 0
    combined = jnp.concatenate(
        [jnp.where(first, own, other), jnp.where(first, other, own)], axis=0
    )
    new_ref[...] = updated(combined, pair_ref[...], gate_w_ref, out_w_ref).reshape(new_ref.shape)


def on_device(
    alignment,
    pair_features,
    query_matrix,
    key_matrix,
    value_matrix,
    gate_matrix,
    output_matrix,
    bias_weight,
    left_factor_weight,
    right_factor_weight,
    outer_weight,
    outgoing_project,
    outgoing_gate,
    outgoing_output,
    incoming_project,
    incoming_gate,
    incoming_output,
):
    seqs, rows, channels = alignment.shape
    cols, depth = pair_features.shape[1:]
    heads = bias_weight.shape[1]
    factor = left_factor_weight.shape[1]
    places = rows * cols
    full = COLS * cols
    core, x_hi = lax.axis_index("core"), lax.axis_index("xh")

    bias = kernel_call(
        functools.partial(bias_kernel, rows), [((cols, heads * rows), BF16)], (pair_features, bias_weight.T)
    )[0]
    chunks = kernel_call(normed_kernel, [((ROWS, seqs, rows, channels), BF16)], (alignment,))[0]
    everyone = exchange(chunks, ROW_X_FIRST)
    bias, query_matrix = from_col(bias, query_matrix)
    queries, gates = kernel_call(
        query_kernel,
        [((seqs, rows, channels), BF16), ((seqs * rows, channels), F32)],
        (alignment, query_matrix, gate_matrix),
    )
    new_alignment, left, right = kernel_call(
        functools.partial(attention_kernel, heads),
        [
            ((seqs, rows, channels), BF16),
            ((seqs, rows * factor), BF16),
            ((ROWS, seqs, rows * factor), BF16),
        ],
        (
            everyone, bias.reshape(full, heads * rows), queries, gates, alignment, key_matrix,
            value_matrix, output_matrix, left_factor_weight.T, right_factor_weight.T,
        ),
        scratch=[((seqs * rows, channels), BF16), ((seqs * rows, 128), F32)],
    )

    size = (rows + cols) * factor
    chunks = kernel_call(
        factor_kernel, [((COLS, seqs, size), BF16)], (left, exchange(right, ROW_X_FIRST))
    )[0]
    factors = exchange(chunks, COL_X_FIRST).reshape(COLS * seqs, size)
    pair_one, left_edge, right_edge = kernel_call(
        outer_kernel,
        [((places, depth), BF16), ((rows, cols, depth), BF16), ((2, cols, cols, depth), BF16)],
        (factors, pair_features, outer_weight, outgoing_project),
        scratch=[
            ((cols * factor // 128, rows * factor, 128), F32),
            ((places, depth), F32),
            ((places, depth), F32),
        ],
    )

    mine = lax.dynamic_index_in_dim(right_edge, core, 0, keepdims=False)
    theirs = lax.dynamic_index_in_dim(right_edge, 1 - core, 0, keepdims=False)
    swapped = flip(jnp.concatenate([left_edge, theirs], axis=0), "core")
    chunks = kernel_call(
        tile_kernel, [((SIZES["z"], 2 * cols, cols, depth), BF16)], (mine, swapped[rows:])
    )[0]
    tiles = exchange(chunks, "z")
    lines = jnp.concatenate([left_edge, swapped[:rows]], axis=1)
    lines = in_order(x_hi, lines, flip(lines, "xh"))
    partial = partial_sums(tiles, lines).reshape(ROWS, rows, cols, depth)
    partial = exchange(partial, ("xl", "y"))
    pair_two, chunks, lines = kernel_call(
        middle_kernel,
        [
            ((places, depth), BF16),
            ((SIZES["y"], rows, cols, depth), BF16),
            ((cols, rows, depth), BF16),
        ],
        (partial, cross(pair_one), outgoing_gate, outgoing_output, incoming_project),
        scratch=[((places, depth), F32)],
    )

    own = exchange(chunks, "y")
    lines = in_order(x_hi, lines, flip(lines, "xh"))
    other = flip(own, "core")
    partial = partial_sums(other, lines, partial_sums(own, lines))
    partial = exchange(partial.reshape(ROWS, 2, cols, cols, depth), ("xl", "z"))
    new_pair = kernel_call(
        last_kernel,
        [((rows, cols, depth), BF16)],
        (jnp.full((8, depth), core), partial, cross(pair_two), incoming_gate, incoming_output),
        scratch=[((places, depth), F32)],
    )[0]
    return (new_alignment, new_pair)


def solution(mesh):
    fine = jax.sharding.Mesh(mesh.devices.reshape(tuple(SIZES.values())), tuple(SIZES))
    rep = (P(),) * 15
    return jax.shard_map(
        on_device,
        mesh=fine,
        in_specs=(P(COL, ROW, None), P(ROW, COL, None)) + rep,
        out_specs=(P(COL, ROW, None), P(ROW, COL, None)),
        check_vma=False,
    )
```

```python
import functools

import jax
import jax.numpy as jnp
from jax import lax
from jax.experimental import pallas as pl
from jax.experimental.pallas import tpu as pltpu
from jax.sharding import PartitionSpec as P

F32 = jnp.float32
BF16 = jnp.bfloat16
ROWS, COLS = 16, 32
SIZES = {"z": 8, "xh": 2, "y": 8, "xl": 2, "core": 2}
ROW, COL = ("z", "xh"), ("y", "xl", "core")
ROW_X_FIRST, COL_X_FIRST = ("xh", "z"), ("core", "xl", "y")
FLIP = [(0, 1), (1, 0)]
CROSS = [(0, 0), (1, 2), (2, 1), (3, 3)]


def layer_norm(values):
    values = values.astype(F32)
    center = values - jnp.mean(values, axis=-1, keepdims=True)
    variance = jnp.mean(center * center, axis=-1, keepdims=True)
    return center * lax.rsqrt(variance + 1e-05)


def sigmoid(values):
    return 1.0 / (1.0 + jnp.exp(-values))


def project(values, weight):
    return jnp.dot(values, weight, preferred_element_type=F32)


def exchange(chunks, axes):
    return lax.all_to_all(chunks, axes, 0, 0)


def flip(block, axis):
    return lax.ppermute(block, axis, FLIP)


def cross(block):
    return lax.ppermute(block, ("xh", "xl"), CROSS)


def in_order(place, own, other, axis=0):
    lower = jnp.where(place == 0, own, other)
    upper = jnp.where(place == 0, other, own)
    return jnp.concatenate([lower, upper], axis=axis)


def kernel_call(body, outs, args, scratch=(), flops=0, fetched=False):
    shapes = [jax.ShapeDtypeStruct(s, d) for s, d in outs]
    vmem = pl.BlockSpec(memory_space=pltpu.VMEM)
    size = sum(a.size * a.dtype.itemsize for a in args)
    size += sum(s.size * jnp.dtype(s.dtype).itemsize for s in shapes)
    return pl.pallas_call(
        body,
        out_shape=shapes,
        in_specs=[pl.BlockSpec() if fetched else vmem] * len(args),
        out_specs=[vmem] * len(shapes),
        scratch_shapes=[pltpu.VMEM(s, d) for s, d in scratch],
        compiler_params=pltpu.CompilerParams(vmem_limit_bytes=40 * 2**20),
        cost_estimate=pl.CostEstimate(flops=flops, bytes_accessed=size, transcendentals=0),
    )(*args)


def shifted(block, step):
    size = SIZES["y"]
    return lax.ppermute(block, "y", [(y, (y - step) % size) for y in range(size)])


def from_col(block, later):
    held = block[None, None, None]
    held = in_order(lax.axis_index("core"), held, flip(held, "core"), 2)
    held, later = lax.optimization_barrier((held, later))
    near = jnp.concatenate([shifted(held, -1), held, shifted(held, 1)], axis=1)
    far = jnp.concatenate([shifted(near[:, 1:], -3), near, shifted(near, 3)], axis=1)
    size = SIZES["y"]
    start = lax.rem(size + 3 - lax.axis_index("y"), size)
    held = lax.dynamic_slice_in_dim(jnp.concatenate([far, far], axis=1), start, size, 1)
    return in_order(lax.axis_index("xl"), held, flip(held, "xl"), 0), later


def normed_kernel(x_ref, chunks_ref):
    normed = layer_norm(x_ref[...]).astype(BF16)
    for member in range(chunks_ref.shape[0]):
        chunks_ref[member] = normed


def bias_kernel(rows, pair_ref, bias_w_ref, bias_ref):
    height, width, depth = pair_ref.shape
    heads = bias_w_ref.shape[0]
    pair_normed = layer_norm(pair_ref[...].reshape(height * width, depth)).astype(BF16)
    wide = jnp.concatenate(
        [jnp.broadcast_to(bias_w_ref[h : h + 1, :], (rows, depth)) for h in range(heads)], axis=0
    )
    every = lax.dot_general(
        pair_normed, wide, (((1,), (1,)), ((), ())), preferred_element_type=F32
    ).reshape(height, width, heads * rows)
    lane = lax.broadcasted_iota(jnp.int32, (width, heads * rows), 1) % rows
    bias = jnp.zeros((width, heads * rows), F32)
    for i in range(height):
        bias = jnp.where(lane == i, every[i], bias)
    bias_ref[...] = bias.astype(BF16)


def query_kernel(x_ref, query_w_ref, gate_w_ref, query_ref, gate_ref):
    seqs, rows, channels = x_ref.shape
    normed = layer_norm(x_ref[...].reshape(seqs * rows, channels)).astype(BF16)
    query_ref[...] = project(normed, query_w_ref[...]).astype(BF16).reshape(seqs, rows, channels)
    gate_ref[...] = sigmoid(project(normed, gate_w_ref[...]))


def attention_kernel(
    heads, every_ref, bias_ref, query_ref, gate_ref, x_ref, key_w_ref, value_w_ref, out_w_ref,
    left_w_ref, right_w_ref, new_ref, left_ref, right_ref, gated_ref, factor_ref,
):
    members, seqs, rows, channels = every_ref.shape
    head_dim = channels // heads
    full = members * rows
    bias = bias_ref[...].astype(F32).T
    head_of = lax.broadcasted_iota(jnp.int32, (rows, channels), 1) // head_dim

    def one(s, carry):
        tokens = every_ref[:, s].reshape(full, channels)
        keys = project(tokens, key_w_ref[...]).astype(BF16)
        values = project(tokens, value_w_ref[...]).astype(BF16)
        query = query_ref[s]
        spread_query = jnp.concatenate(
            [jnp.where(head_of == h, query, jnp.zeros_like(query)) for h in range(heads)], axis=0
        )
        scores = lax.dot_general(
            spread_query, keys, (((1,), (1,)), ((), ())), preferred_element_type=F32
        )
        scores = scores * head_dim ** (-0.5) + bias
        expo = jnp.exp(scores - jnp.max(scores, axis=-1, keepdims=True))
        weights = (expo / jnp.sum(expo, axis=-1, keepdims=True)).astype(BF16)
        mixed = project(weights, values)
        attended = mixed[0:rows]
        for h in range(1, heads):
            attended = jnp.where(head_of == h, mixed[h * rows : (h + 1) * rows], attended)
        place = pl.ds(pl.multiple_of(s * rows, rows), rows)
        gated_ref[place, :] = (gate_ref[place, :] * attended).astype(BF16)
        return carry

    lax.fori_loop(0, seqs, one, 0, unroll=True)
    tokens = x_ref[...].reshape(seqs * rows, channels).astype(F32)
    new = (tokens + project(gated_ref[...], out_w_ref[...])).astype(BF16)
    new_ref[...] = new.reshape(seqs, rows, channels)
    width = left_w_ref.shape[0]
    factor_w = jnp.concatenate([left_w_ref[...], right_w_ref[...]], axis=0)
    factor_ref[:, : 2 * width] = lax.dot_general(
        layer_norm(new).astype(BF16), factor_w, (((1,), (1,)), ((), ())), preferred_element_type=F32
    )
    pieces = [factor_ref[pl.ds(i, seqs, stride=rows), :] for i in range(rows)]
    left_ref[...] = jnp.concatenate([p[:, :width] for p in pieces], axis=1).astype(BF16)
    right = jnp.concatenate([p[:, width : 2 * width] for p in pieces], axis=1).astype(BF16)
    for member in range(right_ref.shape[0]):
        right_ref[member] = right


def factor_kernel(left_ref, right_ref, chunks_ref):
    members, _, size = right_ref.shape
    pieces = chunks_ref.shape[0] // members
    split = size // pieces
    left = left_ref[...]
    for place in range(chunks_ref.shape[0]):
        part = place // members
        chunks_ref[place, :, : left.shape[1]] = left
        chunks_ref[place, :, left.shape[1] :] = right_ref[
            place % members, :, part * split : (part + 1) * split
        ]


def edge_parts(pair, in_w_ref):
    normed = layer_norm(pair).astype(BF16)
    proj = project(normed, in_w_ref[...])
    width = in_w_ref.shape[1] // 4
    left = sigmoid(proj[:, :width]) * proj[:, width : 2 * width]
    right = sigmoid(proj[:, 2 * width : 3 * width]) * proj[:, 3 * width :]
    return left, right


def updated(combined, pair, gate_w_ref, out_w_ref):
    gate = sigmoid(project(layer_norm(pair).astype(BF16), gate_w_ref[...]))
    update = project(layer_norm(combined).astype(BF16), out_w_ref[...])
    return (pair.astype(F32) + gate * update).astype(BF16)


def outer_kernel(
    factors_ref, pair_ref, outer_w_ref, in_w_ref,
    pair_out, left_out, right_out, products_ref, update_ref, right_scr,
):
    total, size = factors_ref.shape
    rows, cols, depth = pair_ref.shape
    factor = size // (rows + cols)
    products = lax.dot_general(
        factors_ref[:, : rows * factor], factors_ref[:, rows * factor :], (((0,), (0,)), ((), ())), preferred_element_type=F32
    ) * (1.0 / total)
    slabs, _, slab = products_ref.shape
    per_slab = slab // factor
    outer = []
    for part in range(slabs):
        products_ref[part] = products[:, part * slab : (part + 1) * slab]
        lines = [
            products_ref[part, pl.ds(a, rows, stride=factor), :].astype(BF16) for a in range(factor)
        ]
        for j in range(per_slab):
            pieces = [line[:, j * factor : (j + 1) * factor] for line in lines]
            outer.append(jnp.concatenate(pieces, axis=1))
    outer = jnp.concatenate(outer, axis=0)
    update_ref[...] = project(outer, outer_w_ref[...])
    update = jnp.concatenate(
        [update_ref[pl.ds(i, cols, stride=rows), :] for i in range(rows)], axis=0
    )
    pair = (pair_ref[...].reshape(rows * cols, depth).astype(F32) + update).astype(BF16)
    pair_out[...] = pair
    left, right = edge_parts(pair, in_w_ref)
    left_out[...] = left.astype(BF16).reshape(rows, cols, depth)
    right_scr[...] = right
    for k in range(cols):
        line = right_scr[pl.ds(k, rows, stride=cols), :].astype(BF16)
        for half in range(right_out.shape[0]):
            for member in range(right_out.shape[1]):
                right_out[half, member, k] = line[half * cols : (half + 1) * cols]


def partial_kernel(tile_ref, line_ref, *refs):
    before_ref, out_ref, scr = refs if len(refs) == 3 else (None,) + refs
    sides, groups, side = tile_ref.shape[:3]
    depth = sides * side
    scr[...] = line_ref[...].astype(F32)
    per_part = out_ref.shape[-3]

    def one(g, carry):
        tiles = [
            [tile_ref[k // side, 2 * g + u, k % side].astype(F32) for k in range(depth)]
            for u in range(2)
        ]
        for n in range(line_ref.shape[0]):
            part, place = divmod(n, per_part)
            totals = [None, None]
            for k in range(depth):
                line = scr[n, k : k + 1, :]
                for u in range(2):
                    term = tiles[u][k] * line
                    totals[u] = term if k == 0 else totals[u] + term
            for u in range(2):
                if before_ref is None:
                    out_ref[part, 2 * g + u, place] = totals[u].astype(BF16)
                else:
                    out_ref[part, 2 * g + u, 0, place] = before_ref[part, 2 * g + u, place]
                    out_ref[part, 2 * g + u, 1, place] = totals[u].astype(BF16)
        return carry

    lax.fori_loop(0, groups // 2, one, 0)


def partial_sums(tiles, lines, before=None):
    _, groups, _, height, width = tiles.shape
    count, depth = lines.shape[:2]
    beside = () if before is None else (2,)
    return kernel_call(
        partial_kernel,
        [((2, groups) + beside + (count // 2, height, width), BF16)],
        (tiles, lines) if before is None else (tiles, lines, before),
        scratch=[((count, depth, width), F32)],
        flops=2 * groups * count * height * width * depth,
    )[0]


def added(partial_ref):
    total = partial_ref[0].astype(F32)
    for member in range(1, partial_ref.shape[0]):
        total = total + partial_ref[member].astype(F32)
    return total


def middle_kernel(
    partial_ref, pair_ref, gate_w_ref, out_w_ref, in_w_ref, pair_out, chunks_out, line_out, right_scr
):
    rows, cols, depth = partial_ref.shape[1:]
    combined = added(partial_ref).reshape(rows * cols, depth)
    pair = updated(combined, pair_ref[...], gate_w_ref, out_w_ref)
    pair_out[...] = pair
    left, right = edge_parts(pair, in_w_ref)
    left = left.astype(BF16).reshape(rows, cols, depth)
    for member in range(chunks_out.shape[0]):
        chunks_out[member] = left
    right_scr[...] = right
    for j in range(cols):
        line_out[j] = right_scr[pl.ds(j, rows, stride=cols), :].astype(BF16)


def last_kernel(core_ref, partial_ref, pair_ref, gate_w_ref, out_w_ref, new_ref, scr):
    halves, cols, tall, depth = partial_ref.shape[1:]
    scr[...] = added(partial_ref).reshape(halves * cols * tall, depth)
    own, other = [
        jnp.concatenate(
            [scr[pl.ds(half * cols * tall + i, cols, stride=tall), :] for i in range(tall)], axis=0
        )
        for half in range(halves)
    ]
    first = core_ref[0:1, :] == 0
    combined = jnp.concatenate(
        [jnp.where(first, own, other), jnp.where(first, other, own)], axis=0
    )
    new_ref[...] = updated(combined, pair_ref[...], gate_w_ref, out_w_ref).reshape(new_ref.shape)


def on_device(
    alignment,
    pair_features,
    query_matrix,
    key_matrix,
    value_matrix,
    gate_matrix,
    output_matrix,
    bias_weight,
    left_factor_weight,
    right_factor_weight,
    outer_weight,
    outgoing_project,
    outgoing_gate,
    outgoing_output,
    incoming_project,
    incoming_gate,
    incoming_output,
):
    seqs, rows, channels = alignment.shape
    cols, depth = pair_features.shape[1:]
    heads = bias_weight.shape[1]
    factor = left_factor_weight.shape[1]
    places = rows * cols
    full = COLS * cols
    core, x_hi = lax.axis_index("core"), lax.axis_index("xh")

    chunks = kernel_call(
        normed_kernel, [((ROWS, seqs, rows, channels), BF16)], (alignment,), fetched=True
    )[0]
    chunks, later_pair = lax.optimization_barrier((chunks, pair_features))
    bias = kernel_call(
        functools.partial(bias_kernel, rows),
        [((cols, heads * rows), BF16)],
        (later_pair, bias_weight.T),
        fetched=True,
    )[0]
    everyone = exchange(chunks, ROW_X_FIRST)
    bias, query_matrix = from_col(bias, query_matrix)
    queries, gates = kernel_call(
        query_kernel,
        [((seqs, rows, channels), BF16), ((seqs * rows, channels), F32)],
        (alignment, query_matrix, gate_matrix),
    )
    new_alignment, left, right = kernel_call(
        functools.partial(attention_kernel, heads),
        [
            ((seqs, rows, channels), BF16),
            ((seqs, rows * factor), BF16),
            ((ROWS, seqs, rows * factor), BF16),
        ],
        (
            everyone, bias.reshape(full, heads * rows), queries, gates, alignment, key_matrix,
            value_matrix, output_matrix, left_factor_weight.T, right_factor_weight.T,
        ),
        scratch=[((seqs * rows, channels), BF16), ((seqs * rows, 128), F32)],
    )

    size = (rows + cols) * factor
    chunks = kernel_call(
        factor_kernel, [((COLS, seqs, size), BF16)], (left, exchange(right, ROW_X_FIRST))
    )[0]
    factors = exchange(chunks, COL_X_FIRST).reshape(COLS * seqs, size)
    pair_one, left_edge, right_edge = kernel_call(
        outer_kernel,
        [((places, depth), BF16), ((rows, cols, depth), BF16), ((2, SIZES["z"], cols, cols, depth), BF16)],
        (factors, pair_features, outer_weight, outgoing_project),
        scratch=[
            ((cols * factor // 128, rows * factor, 128), F32),
            ((places, depth), F32),
            ((places, depth), F32),
        ],
    )

    chunks = right_edge.reshape((ROWS,) + right_edge.shape[2:])
    tiles = exchange(chunks, ("core", "z")).reshape(right_edge.shape)
    lines = in_order(core, left_edge, flip(left_edge, "core"), axis=1)
    lines = in_order(x_hi, lines, flip(lines, "xh"))
    partial = partial_sums(tiles, lines).reshape(ROWS, rows, cols, depth)
    partial = exchange(partial, ("xl", "y"))
    pair_two, chunks, lines = kernel_call(
        middle_kernel,
        [
            ((places, depth), BF16),
            ((SIZES["y"], rows, cols, depth), BF16),
            ((cols, rows, depth), BF16),
        ],
        (partial, cross(pair_one), outgoing_gate, outgoing_output, incoming_project),
        scratch=[((places, depth), F32)],
    )

    own = exchange(chunks, "y")
    lines = in_order(x_hi, lines, flip(lines, "xh"))
    other = flip(own, "core")
    partial = partial_sums(other[None], lines, partial_sums(own[None], lines))
    partial = exchange(partial.reshape(ROWS, 2, cols, cols, depth), ("xl", "z"))
    new_pair = kernel_call(
        last_kernel,
        [((rows, cols, depth), BF16)],
        (jnp.full((8, depth), core), partial, cross(pair_two), incoming_gate, incoming_output),
        scratch=[((places, depth), F32)],
    )[0]
    return (new_alignment, new_pair)


def solution(mesh):
    fine = jax.sharding.Mesh(mesh.devices.reshape(tuple(SIZES.values())), tuple(SIZES))
    rep = (P(),) * 15
    return jax.shard_map(
        on_device,
        mesh=fine,
        in_specs=(P(COL, ROW, None), P(ROW, COL, None)) + rep,
        out_specs=(P(COL, ROW, None), P(ROW, COL, None)),
        check_vma=False,
    )
```

```python
import functools

import jax
import jax.numpy as jnp
from jax import lax
from jax.experimental import pallas as pl
from jax.experimental.pallas import tpu as pltpu
from jax.sharding import PartitionSpec as P

F32 = jnp.float32
BF16 = jnp.bfloat16
ROWS, COLS = 16, 32
SIZES = {"z": 8, "xh": 2, "y": 8, "xl": 2, "core": 2}
ROW, COL = ("z", "xh"), ("y", "xl", "core")
ROW_X_FIRST, COL_X_FIRST = ("xh", "z"), ("xl", "core", "y")
FLIP = [(0, 1), (1, 0)]
CROSS = [(0, 0), (1, 2), (2, 1), (3, 3)]


def layer_norm(values):
    values = values.astype(F32)
    center = values - jnp.mean(values, axis=-1, keepdims=True)
    variance = jnp.mean(center * center, axis=-1, keepdims=True)
    return center * lax.rsqrt(variance + 1e-05)


def sigmoid(values):
    return 1.0 / (1.0 + jnp.exp(-values))


def project(values, weight):
    return jnp.dot(values, weight, preferred_element_type=F32)


def exchange(chunks, axes):
    return lax.all_to_all(chunks, axes, 0, 0)


def flip(block, axis):
    return lax.ppermute(block, axis, FLIP)


def cross(block):
    return lax.ppermute(block, ("xh", "xl"), CROSS)


def in_order(place, own, other, axis=0):
    lower = jnp.where(place == 0, own, other)
    upper = jnp.where(place == 0, other, own)
    return jnp.concatenate([lower, upper], axis=axis)


def kernel_call(body, outs, args, scratch=(), flops=0, fetched=False):
    shapes = [jax.ShapeDtypeStruct(s, d) for s, d in outs]
    vmem = pl.BlockSpec(memory_space=pltpu.VMEM)
    size = sum(a.size * a.dtype.itemsize for a in args)
    size += sum(s.size * jnp.dtype(s.dtype).itemsize for s in shapes)
    return pl.pallas_call(
        body,
        out_shape=shapes,
        in_specs=[pl.BlockSpec() if fetched else vmem] * len(args),
        out_specs=[vmem] * len(shapes),
        scratch_shapes=[pltpu.VMEM(s, d) for s, d in scratch],
        compiler_params=pltpu.CompilerParams(vmem_limit_bytes=40 * 2**20),
        cost_estimate=pl.CostEstimate(flops=flops, bytes_accessed=size, transcendentals=0),
    )(*args)


def shifted(block, step):
    size = SIZES["y"]
    return lax.ppermute(block, "y", [(y, (y - step) % size) for y in range(size)])


def from_col(block, later):
    held = block[None, None, None]
    held = in_order(lax.axis_index("core"), held, flip(held, "core"), 2)
    held, later = lax.optimization_barrier((held, later))
    near = jnp.concatenate([shifted(held, -1), held, shifted(held, 1)], axis=1)
    far = jnp.concatenate([shifted(near[:, 1:], -3), near, shifted(near, 3)], axis=1)
    size = SIZES["y"]
    start = lax.rem(size + 3 - lax.axis_index("y"), size)
    held = lax.dynamic_slice_in_dim(jnp.concatenate([far, far], axis=1), start, size, 1)
    return in_order(lax.axis_index("xl"), held, flip(held, "xl"), 0), later


def normed_kernel(x_ref, chunks_ref):
    normed = layer_norm(x_ref[...]).astype(BF16)
    for member in range(chunks_ref.shape[0]):
        chunks_ref[member] = normed


def bias_kernel(rows, pair_ref, bias_w_ref, bias_ref):
    height, width, depth = pair_ref.shape
    heads = bias_w_ref.shape[0]
    weight = bias_w_ref[...].astype(F32)
    pair_normed = layer_norm(pair_ref[...].astype(F32).reshape(height * width, depth)).astype(BF16)
    wide = jnp.concatenate(
        [jnp.broadcast_to(weight[h : h + 1, :], (rows, depth)) for h in range(heads)], axis=0
    ).astype(BF16)
    every = lax.dot_general(
        pair_normed, wide, (((1,), (1,)), ((), ())), preferred_element_type=F32
    ).reshape(height, width, heads * rows)
    lane = lax.broadcasted_iota(jnp.int32, (width, heads * rows), 1) % rows
    bias = jnp.zeros((width, heads * rows), F32)
    for i in range(height):
        bias = jnp.where(lane == i, every[i], bias)
    bias_ref[...] = bias.astype(BF16)


def query_kernel(x_ref, query_w_ref, gate_w_ref, query_ref, gate_ref):
    seqs, rows, channels = x_ref.shape
    normed = layer_norm(x_ref[...].reshape(seqs * rows, channels)).astype(BF16)
    query_ref[...] = project(normed, query_w_ref[...]).astype(BF16).reshape(seqs, rows, channels)
    gate_ref[...] = sigmoid(project(normed, gate_w_ref[...]))


def attention_kernel(
    heads, every_ref, bias_ref, query_ref, gate_ref, x_ref, key_w_ref, value_w_ref, out_w_ref,
    left_w_ref, right_w_ref, new_ref, left_ref, right_ref, gated_ref, factor_ref,
):
    members, seqs, rows, channels = every_ref.shape
    head_dim = channels // heads
    full = members * rows
    bias = bias_ref[...].astype(F32).T
    head_of = lax.broadcasted_iota(jnp.int32, (rows, channels), 1) // head_dim

    def one(s, carry):
        tokens = every_ref[:, s].reshape(full, channels)
        keys = project(tokens, key_w_ref[...]).astype(BF16)
        values = project(tokens, value_w_ref[...]).astype(BF16)
        query = query_ref[s]
        spread_query = jnp.concatenate(
            [jnp.where(head_of == h, query, jnp.zeros_like(query)) for h in range(heads)], axis=0
        )
        scores = lax.dot_general(
            spread_query, keys, (((1,), (1,)), ((), ())), preferred_element_type=F32
        )
        scores = scores * head_dim ** (-0.5) + bias
        expo = jnp.exp(scores - jnp.max(scores, axis=-1, keepdims=True))
        weights = (expo / jnp.sum(expo, axis=-1, keepdims=True)).astype(BF16)
        mixed = project(weights, values)
        attended = mixed[0:rows]
        for h in range(1, heads):
            attended = jnp.where(head_of == h, mixed[h * rows : (h + 1) * rows], attended)
        place = pl.ds(pl.multiple_of(s * rows, rows), rows)
        gated_ref[place, :] = (gate_ref[place, :] * attended).astype(BF16)
        return carry

    lax.fori_loop(0, seqs, one, 0, unroll=True)
    tokens = x_ref[...].reshape(seqs * rows, channels).astype(F32)
    new = (tokens + project(gated_ref[...], out_w_ref[...])).astype(BF16)
    new_ref[...] = new.reshape(seqs, rows, channels)
    width = left_w_ref.shape[0]
    factor_w = jnp.concatenate([left_w_ref[...], right_w_ref[...]], axis=0)
    factor_ref[:, : 2 * width] = lax.dot_general(
        layer_norm(new).astype(BF16), factor_w, (((1,), (1,)), ((), ())), preferred_element_type=F32
    )
    pieces = [factor_ref[pl.ds(i, seqs, stride=rows), :] for i in range(rows)]
    left_ref[...] = jnp.concatenate([p[:, :width] for p in pieces], axis=1).astype(BF16)
    right = jnp.concatenate([p[:, width : 2 * width] for p in pieces], axis=1).astype(BF16)
    for member in range(right_ref.shape[0]):
        right_ref[member] = right


def factor_kernel(left_ref, right_ref, chunks_ref):
    members, _, size = right_ref.shape
    split = size // 2
    left = left_ref[...]
    for place in range(chunks_ref.shape[0]):
        x_lo, part, y = place // members, place // SIZES["y"] % 2, place % SIZES["y"]
        chunks_ref[place, :, : left.shape[1]] = left
        chunks_ref[place, :, left.shape[1] :] = right_ref[
            x_lo * SIZES["y"] + y, :, part * split : (part + 1) * split
        ]


def edge_parts(pair, in_w_ref):
    normed = layer_norm(pair).astype(BF16)
    proj = project(normed, in_w_ref[...])
    width = in_w_ref.shape[1] // 4
    left = sigmoid(proj[:, :width]) * proj[:, width : 2 * width]
    right = sigmoid(proj[:, 2 * width : 3 * width]) * proj[:, 3 * width :]
    return left, right


def updated(combined, pair, gate_w_ref, out_w_ref):
    gate = sigmoid(project(layer_norm(pair).astype(BF16), gate_w_ref[...]))
    update = project(layer_norm(combined).astype(BF16), out_w_ref[...])
    return (pair.astype(F32) + gate * update).astype(BF16)


def outer_kernel(
    factors_ref, pair_ref, outer_w_ref, in_w_ref,
    pair_out, left_out, right_out, products_ref, update_ref, right_scr,
):
    total, size = factors_ref.shape
    rows, cols, depth = pair_ref.shape
    factor = size // (rows + cols)
    products = lax.dot_general(
        factors_ref[:, : rows * factor], factors_ref[:, rows * factor :], (((0,), (0,)), ((), ())), preferred_element_type=F32
    ) * (1.0 / total)
    slabs, _, slab = products_ref.shape
    per_slab = slab // factor
    outer = []
    for part in range(slabs):
        products_ref[part] = products[:, part * slab : (part + 1) * slab]
        lines = [
            products_ref[part, pl.ds(a, rows, stride=factor), :].astype(BF16) for a in range(factor)
        ]
        for j in range(per_slab):
            pieces = [line[:, j * factor : (j + 1) * factor] for line in lines]
            outer.append(jnp.concatenate(pieces, axis=1))
    outer = jnp.concatenate(outer, axis=0)
    update_ref[...] = project(outer, outer_w_ref[...])
    update = jnp.concatenate(
        [update_ref[pl.ds(i, cols, stride=rows), :] for i in range(rows)], axis=0
    )
    pair = (pair_ref[...].astype(F32).reshape(rows * cols, depth) + update).astype(BF16)
    pair_out[...] = pair
    left, right = edge_parts(pair, in_w_ref)
    left_out[...] = left.reshape(rows, cols, depth).astype(BF16)
    right_scr[...] = right
    for k in range(cols):
        line = right_scr[pl.ds(k, rows, stride=cols), :]
        for half in range(right_out.shape[0]):
            part = line[half * cols : (half + 1) * cols].astype(BF16)
            for member in range(right_out.shape[1]):
                right_out[half, member, k] = part


def partial_kernel(tile_ref, line_ref, *refs):
    before_ref, out_ref, scr = refs if len(refs) == 3 else (None,) + refs
    sides, groups, side = tile_ref.shape[:3]
    depth = sides * side
    scr[...] = line_ref[...].astype(F32)
    per_part = out_ref.shape[-3]

    def one(g, carry):
        tiles = [
            [tile_ref[k // side, 2 * g + u, k % side].astype(F32) for k in range(depth)]
            for u in range(2)
        ]
        for n in range(line_ref.shape[0]):
            part, place = divmod(n, per_part)
            totals = [None, None]
            for k in range(depth):
                line = scr[n, k : k + 1, :]
                for u in range(2):
                    term = tiles[u][k] * line
                    totals[u] = term if k == 0 else totals[u] + term
            for u in range(2):
                if before_ref is None:
                    out_ref[part, 2 * g + u, place] = totals[u].astype(BF16)
                else:
                    out_ref[part, 2 * g + u, 0, place] = before_ref[part, 2 * g + u, place]
                    out_ref[part, 2 * g + u, 1, place] = totals[u].astype(BF16)
        return carry

    lax.fori_loop(0, groups // 2, one, 0)


def partial_sums(tiles, lines, before=None):
    _, groups, _, height, width = tiles.shape
    count, depth = lines.shape[:2]
    beside = () if before is None else (2,)
    return kernel_call(
        partial_kernel,
        [((2, groups) + beside + (count // 2, height, width), BF16)],
        (tiles, lines) if before is None else (tiles, lines, before),
        scratch=[((count, depth, width), F32)],
        flops=2 * groups * count * height * width * depth,
    )[0]


def added(partial_ref):
    total = partial_ref[0].astype(F32)
    for member in range(1, partial_ref.shape[0]):
        total = total + partial_ref[member].astype(F32)
    return total


def middle_kernel(
    partial_ref, pair_ref, gate_w_ref, out_w_ref, in_w_ref, pair_out, chunks_out, line_out, right_scr
):
    rows, cols, depth = partial_ref.shape[1:]
    combined = added(partial_ref).reshape(rows * cols, depth)
    pair = updated(combined, pair_ref[...], gate_w_ref, out_w_ref)
    pair_out[...] = pair
    left, right = edge_parts(pair, in_w_ref)
    left = left.reshape(rows, cols, depth).astype(BF16)
    for member in range(chunks_out.shape[0]):
        chunks_out[member] = left
    right_scr[...] = right
    for j in range(cols):
        line_out[j] = right_scr[pl.ds(j, rows, stride=cols), :].astype(BF16)


def last_kernel(core_ref, partial_ref, pair_ref, gate_w_ref, out_w_ref, new_ref, scr):
    halves, cols, tall, depth = partial_ref.shape[1:]
    scr[...] = added(partial_ref).reshape(halves * cols * tall, depth)
    own, other = [
        jnp.concatenate(
            [scr[pl.ds(half * cols * tall + i, cols, stride=tall), :] for i in range(tall)], axis=0
        )
        for half in range(halves)
    ]
    first = core_ref[0:1, :] == 0
    combined = jnp.concatenate(
        [jnp.where(first, own, other), jnp.where(first, other, own)], axis=0
    )
    new = updated(combined, pair_ref[...], gate_w_ref, out_w_ref)
    new_ref[...] = new.astype(F32).reshape(new_ref.shape).astype(BF16)


def on_device(
    alignment,
    pair_features,
    query_matrix,
    key_matrix,
    value_matrix,
    gate_matrix,
    output_matrix,
    bias_weight,
    left_factor_weight,
    right_factor_weight,
    outer_weight,
    outgoing_project,
    outgoing_gate,
    outgoing_output,
    incoming_project,
    incoming_gate,
    incoming_output,
):
    seqs, rows, channels = alignment.shape
    cols, depth = pair_features.shape[1:]
    heads = bias_weight.shape[1]
    factor = left_factor_weight.shape[1]
    places = rows * cols
    full = COLS * cols
    core, x_hi = lax.axis_index("core"), lax.axis_index("xh")

    chunks = kernel_call(
        normed_kernel, [((ROWS, seqs, rows, channels), BF16)], (alignment,), fetched=True
    )[0]
    chunks, later_pair = lax.optimization_barrier((chunks, pair_features))
    bias = kernel_call(
        functools.partial(bias_kernel, rows),
        [((cols, heads * rows), BF16)],
        (later_pair, bias_weight.T),
        fetched=True,
    )[0]
    everyone = exchange(chunks, ROW_X_FIRST)
    bias, query_matrix = from_col(bias, query_matrix)
    queries, gates = kernel_call(
        query_kernel,
        [((seqs, rows, channels), BF16), ((seqs * rows, channels), F32)],
        (alignment, query_matrix, gate_matrix),
    )
    new_alignment, left, right = kernel_call(
        functools.partial(attention_kernel, heads),
        [
            ((seqs, rows, channels), BF16),
            ((seqs, rows * factor), BF16),
            ((ROWS, seqs, rows * factor), BF16),
        ],
        (
            everyone, bias.reshape(full, heads * rows), queries, gates, alignment, key_matrix,
            value_matrix, output_matrix, left_factor_weight.T, right_factor_weight.T,
        ),
        scratch=[((seqs * rows, channels), BF16), ((seqs * rows, 128), F32)],
    )

    size = (rows + cols) * factor
    chunks = kernel_call(
        factor_kernel, [((COLS, seqs, size), BF16)], (left, exchange(right, ROW_X_FIRST))
    )[0]
    factors = exchange(chunks, COL_X_FIRST).reshape(COLS * seqs, size)
    pair_one, left_edge, right_edge = kernel_call(
        outer_kernel,
        [((places, depth), BF16), ((rows, cols, depth), BF16), ((2, SIZES["z"], cols, cols, depth), BF16)],
        (factors, pair_features, outer_weight, outgoing_project),
        scratch=[
            ((cols * factor // 128, rows * factor, 128), F32),
            ((places, depth), F32),
            ((places, depth), F32),
        ],
    )

    chunks = right_edge.reshape((ROWS,) + right_edge.shape[2:])
    tiles = exchange(chunks, ("core", "z")).reshape(right_edge.shape)
    lines = in_order(core, left_edge, flip(left_edge, "core"), axis=1)
    lines = in_order(x_hi, lines, flip(lines, "xh"))
    partial = partial_sums(tiles, lines).reshape(ROWS, rows, cols, depth)
    partial = exchange(partial, ("xl", "y"))
    pair_two, chunks, lines = kernel_call(
        middle_kernel,
        [
            ((places, depth), BF16),
            ((SIZES["y"], rows, cols, depth), BF16),
            ((cols, rows, depth), BF16),
        ],
        (partial, cross(pair_one), outgoing_gate, outgoing_output, incoming_project),
        scratch=[((places, depth), F32)],
    )

    own = exchange(chunks, "y")
    lines = in_order(x_hi, lines, flip(lines, "xh"))
    other = flip(own, "core")
    partial = partial_sums(other[None], lines, partial_sums(own[None], lines))
    partial = exchange(partial.reshape(ROWS, 2, cols, cols, depth), ("xl", "z"))
    new_pair = kernel_call(
        last_kernel,
        [((rows, cols, depth), BF16)],
        (jnp.full((8, depth), core), partial, cross(pair_two), incoming_gate, incoming_output),
        scratch=[((places, depth), F32)],
    )[0]
    return (new_alignment, new_pair)


def solution(mesh):
    fine = jax.sharding.Mesh(mesh.devices.reshape(tuple(SIZES.values())), tuple(SIZES))
    rep = (P(),) * 15
    return jax.shard_map(
        on_device,
        mesh=fine,
        in_specs=(P(COL, ROW, None), P(ROW, COL, None)) + rep,
        out_specs=(P(COL, ROW, None), P(ROW, COL, None)),
        check_vma=False,
    )
```

```python
import functools

import jax
import jax.numpy as jnp
from jax import lax
from jax.experimental import pallas as pl
from jax.experimental.pallas import tpu as pltpu
from jax.sharding import PartitionSpec as P

F32 = jnp.float32
BF16 = jnp.bfloat16
ROWS, COLS = 16, 32
SIZES = {"z": 8, "xh": 2, "y": 8, "xl": 2, "core": 2}
ROW, COL = ("z", "xh"), ("y", "xl", "core")
ROW_X_FIRST, COL_X_FIRST = ("xh", "z"), ("xl", "core", "y")
FLIP = [(0, 1), (1, 0)]
CROSS = [(0, 0), (1, 2), (2, 1), (3, 3)]


def layer_norm(values):
    values = values.astype(F32)
    center = values - jnp.mean(values, axis=-1, keepdims=True)
    variance = jnp.mean(center * center, axis=-1, keepdims=True)
    return center * lax.rsqrt(variance + 1e-05)


def sigmoid(values):
    return 1.0 / (1.0 + jnp.exp(-values))


def project(values, weight):
    return jnp.dot(values, weight, preferred_element_type=F32)


def exchange(chunks, axes):
    return lax.all_to_all(chunks, axes, 0, 0)


def flip(block, axis):
    return lax.ppermute(block, axis, FLIP)


def cross(block):
    return lax.ppermute(block, ("xh", "xl"), CROSS)


def in_order(place, own, other, axis=0):
    lower = jnp.where(place == 0, own, other)
    upper = jnp.where(place == 0, other, own)
    return jnp.concatenate([lower, upper], axis=axis)


def kernel_call(body, outs, args, scratch=(), flops=0, fetched=False):
    shapes = [jax.ShapeDtypeStruct(s, d) for s, d in outs]
    vmem = pl.BlockSpec(memory_space=pltpu.VMEM)
    size = sum(a.size * a.dtype.itemsize for a in args)
    size += sum(s.size * jnp.dtype(s.dtype).itemsize for s in shapes)
    return pl.pallas_call(
        body,
        out_shape=shapes,
        in_specs=[pl.BlockSpec() if fetched else vmem] * len(args),
        out_specs=[vmem] * len(shapes),
        scratch_shapes=[pltpu.VMEM(s, d) for s, d in scratch],
        compiler_params=pltpu.CompilerParams(vmem_limit_bytes=40 * 2**20),
        cost_estimate=pl.CostEstimate(flops=flops, bytes_accessed=size, transcendentals=0),
    )(*args)


def shifted(block, step):
    size = SIZES["y"]
    return lax.ppermute(block, "y", [(y, (y - step) % size) for y in range(size)])


def from_col(block, later):
    held = block[None, None, None]
    held = in_order(lax.axis_index("core"), held, flip(held, "core"), 2)
    held, later = lax.optimization_barrier((held, later))
    near = jnp.concatenate([shifted(held, -1), held, shifted(held, 1)], axis=1)
    far = jnp.concatenate([shifted(near[:, 1:], -3), near, shifted(near, 3)], axis=1)
    size = SIZES["y"]
    start = lax.rem(size + 3 - lax.axis_index("y"), size)
    held = lax.dynamic_slice_in_dim(jnp.concatenate([far, far], axis=1), start, size, 1)
    return in_order(lax.axis_index("xl"), held, flip(held, "xl"), 0), later


def normed_kernel(x_ref, chunks_ref):
    normed = layer_norm(x_ref[...]).astype(BF16)
    for member in range(chunks_ref.shape[0]):
        chunks_ref[member] = normed


def bias_kernel(rows, pair_ref, bias_w_ref, bias_ref):
    height, width, depth = pair_ref.shape
    heads = bias_w_ref.shape[0]
    weight = bias_w_ref[...].astype(F32)
    pair_normed = layer_norm(pair_ref[...].astype(F32).reshape(height * width, depth)).astype(BF16)
    wide = jnp.concatenate(
        [jnp.broadcast_to(weight[h : h + 1, :], (rows, depth)) for h in range(heads)], axis=0
    ).astype(BF16)
    every = lax.dot_general(
        pair_normed, wide, (((1,), (1,)), ((), ())), preferred_element_type=F32
    ).reshape(height, width, heads * rows)
    lane = lax.broadcasted_iota(jnp.int32, (width, heads * rows), 1) % rows
    bias = jnp.zeros((width, heads * rows), F32)
    for i in range(height):
        bias = jnp.where(lane == i, every[i], bias)
    bias_ref[...] = bias.astype(BF16)


def query_kernel(x_ref, query_w_ref, gate_w_ref, query_ref, gate_ref):
    seqs, rows, channels = x_ref.shape
    normed = layer_norm(x_ref[...].reshape(seqs * rows, channels)).astype(BF16)
    query_ref[...] = project(normed, query_w_ref[...]).astype(BF16).reshape(seqs, rows, channels)
    gate_ref[...] = sigmoid(project(normed, gate_w_ref[...]))


def attention_kernel(
    heads, every_ref, bias_ref, query_ref, gate_ref, x_ref, key_w_ref, value_w_ref, out_w_ref,
    left_w_ref, right_w_ref, new_ref, left_ref, right_ref, gated_ref, factor_ref,
):
    members, seqs, rows, channels = every_ref.shape
    head_dim = channels // heads
    full = members * rows
    bias = bias_ref[...].astype(F32).T
    head_of = lax.broadcasted_iota(jnp.int32, (rows, channels), 1) // head_dim

    def one(s, carry):
        tokens = every_ref[:, s].reshape(full, channels)
        keys = project(tokens, key_w_ref[...]).astype(BF16)
        values = project(tokens, value_w_ref[...]).astype(BF16)
        query = query_ref[s]
        spread_query = jnp.concatenate(
            [jnp.where(head_of == h, query, jnp.zeros_like(query)) for h in range(heads)], axis=0
        )
        scores = lax.dot_general(
            spread_query, keys, (((1,), (1,)), ((), ())), preferred_element_type=F32
        )
        scores = scores * head_dim ** (-0.5) + bias
        expo = jnp.exp(scores - jnp.max(scores, axis=-1, keepdims=True))
        weights = (expo / jnp.sum(expo, axis=-1, keepdims=True)).astype(BF16)
        mixed = project(weights, values)
        attended = mixed[0:rows]
        for h in range(1, heads):
            attended = jnp.where(head_of == h, mixed[h * rows : (h + 1) * rows], attended)
        place = pl.ds(pl.multiple_of(s * rows, rows), rows)
        gated_ref[place, :] = (gate_ref[place, :] * attended).astype(BF16)
        return carry

    lax.fori_loop(0, seqs, one, 0, unroll=True)
    tokens = x_ref[...].reshape(seqs * rows, channels).astype(F32)
    new = (tokens + project(gated_ref[...], out_w_ref[...])).astype(BF16)
    new_ref[...] = new.reshape(seqs, rows, channels)
    width = left_w_ref.shape[0]
    factor_w = jnp.concatenate([left_w_ref[...], right_w_ref[...]], axis=0)
    factor_ref[:, : 2 * width] = lax.dot_general(
        layer_norm(new).astype(BF16), factor_w, (((1,), (1,)), ((), ())), preferred_element_type=F32
    )
    pieces = [factor_ref[pl.ds(i, seqs, stride=rows), :] for i in range(rows)]
    left_ref[...] = jnp.concatenate([p[:, :width] for p in pieces], axis=1).astype(BF16)
    right = jnp.concatenate([p[:, width : 2 * width] for p in pieces], axis=1).astype(BF16)
    for member in range(right_ref.shape[0]):
        right_ref[member] = right


def factor_kernel(left_ref, right_ref, chunks_ref):
    members, _, size = right_ref.shape
    split = size // 2
    left = left_ref[...]
    for place in range(chunks_ref.shape[0]):
        x_lo, part, y = place // members, place // SIZES["y"] % 2, place % SIZES["y"]
        chunks_ref[place, :, : left.shape[1]] = left
        chunks_ref[place, :, left.shape[1] :] = right_ref[
            x_lo * SIZES["y"] + y, :, part * split : (part + 1) * split
        ]


def edge_parts(pair, in_w_ref):
    normed = layer_norm(pair).astype(BF16)
    proj = project(normed, in_w_ref[...])
    width = in_w_ref.shape[1] // 4
    left = sigmoid(proj[:, :width]) * proj[:, width : 2 * width]
    right = sigmoid(proj[:, 2 * width : 3 * width]) * proj[:, 3 * width :]
    return left, right


def pair_gate_kernel(pair_ref, gate_w_ref, gate_ref):
    gate_ref[...] = sigmoid(project(layer_norm(pair_ref[...]).astype(BF16), gate_w_ref[...]))


def pair_gate(pair, weight):
    return kernel_call(pair_gate_kernel, [(pair.shape, F32)], (pair, weight))[0]


def updated(combined, pair, gate, out_w_ref):
    update = project(layer_norm(combined).astype(BF16), out_w_ref[...])
    return (pair.astype(F32) + gate * update).astype(BF16)


def outer_kernel(
    factors_ref, pair_ref, outer_w_ref, in_w_ref,
    pair_out, left_out, right_out, products_ref, update_ref, right_scr,
):
    total, size = factors_ref.shape
    rows, cols, depth = pair_ref.shape
    factor = size // (rows + cols)
    products = lax.dot_general(
        factors_ref[:, : rows * factor], factors_ref[:, rows * factor :], (((0,), (0,)), ((), ())), preferred_element_type=F32
    ) * (1.0 / total)
    slabs, _, slab = products_ref.shape
    per_slab = slab // factor
    outer = []
    for part in range(slabs):
        products_ref[part] = products[:, part * slab : (part + 1) * slab]
        lines = [
            products_ref[part, pl.ds(a, rows, stride=factor), :].astype(BF16) for a in range(factor)
        ]
        for j in range(per_slab):
            pieces = [line[:, j * factor : (j + 1) * factor] for line in lines]
            outer.append(jnp.concatenate(pieces, axis=1))
    outer = jnp.concatenate(outer, axis=0)
    update_ref[...] = project(outer, outer_w_ref[...])
    update = jnp.concatenate(
        [update_ref[pl.ds(i, cols, stride=rows), :] for i in range(rows)], axis=0
    )
    pair = (pair_ref[...].astype(F32).reshape(rows * cols, depth) + update).astype(BF16)
    pair_out[...] = pair
    left, right = edge_parts(pair, in_w_ref)
    left_out[...] = left.reshape(rows, cols, depth).astype(BF16)
    right_scr[...] = right
    for k in range(cols):
        line = right_scr[pl.ds(k, rows, stride=cols), :]
        for half in range(right_out.shape[0]):
            part = line[half * cols : (half + 1) * cols].astype(BF16)
            for member in range(right_out.shape[1]):
                right_out[half, member, k] = part


def partial_kernel(tile_ref, line_ref, *refs):
    before_ref, out_ref, scr = refs if len(refs) == 3 else (None,) + refs
    sides, groups, side = tile_ref.shape[:3]
    depth = sides * side
    scr[...] = line_ref[...].astype(F32)
    per_part = out_ref.shape[-3]

    def one(g, carry):
        tiles = [
            [tile_ref[k // side, 2 * g + u, k % side].astype(F32) for k in range(depth)]
            for u in range(2)
        ]
        for n in range(line_ref.shape[0]):
            part, place = divmod(n, per_part)
            totals = [None, None]
            for k in range(depth):
                line = scr[n, k : k + 1, :]
                for u in range(2):
                    term = tiles[u][k] * line
                    totals[u] = term if k == 0 else totals[u] + term
            for u in range(2):
                if before_ref is None:
                    out_ref[part, 2 * g + u, place] = totals[u].astype(BF16)
                else:
                    out_ref[part, 2 * g + u, 0, place] = before_ref[part, 2 * g + u, place]
                    out_ref[part, 2 * g + u, 1, place] = totals[u].astype(BF16)
        return carry

    lax.fori_loop(0, groups // 2, one, 0, unroll=True)


def partial_sums(tiles, lines, before=None):
    _, groups, _, height, width = tiles.shape
    count, depth = lines.shape[:2]
    beside = () if before is None else (2,)
    return kernel_call(
        partial_kernel,
        [((2, groups) + beside + (count // 2, height, width), BF16)],
        (tiles, lines) if before is None else (tiles, lines, before),
        scratch=[((count, depth, width), F32)],
        flops=2 * groups * count * height * width * depth,
    )[0]


def added(partial_ref):
    total = partial_ref[0].astype(F32)
    for member in range(1, partial_ref.shape[0]):
        total = total + partial_ref[member].astype(F32)
    return total


def middle_kernel(
    partial_ref, pair_ref, gate_ref, out_w_ref, in_w_ref, pair_out, chunks_out, line_out, right_scr
):
    rows, cols, depth = partial_ref.shape[1:]
    combined = added(partial_ref).reshape(rows * cols, depth)
    pair = updated(combined, pair_ref[...], gate_ref[...], out_w_ref)
    pair_out[...] = pair
    left, right = edge_parts(pair, in_w_ref)
    left = left.reshape(rows, cols, depth).astype(BF16)
    for member in range(chunks_out.shape[0]):
        chunks_out[member] = left
    right_scr[...] = right
    for j in range(cols):
        line_out[j] = right_scr[pl.ds(j, rows, stride=cols), :].astype(BF16)


def last_kernel(core_ref, partial_ref, pair_ref, gate_ref, out_w_ref, new_ref, scr):
    halves, cols, tall, depth = partial_ref.shape[1:]
    scr[...] = added(partial_ref).reshape(halves * cols * tall, depth)
    own, other = [
        jnp.concatenate(
            [scr[pl.ds(half * cols * tall + i, cols, stride=tall), :] for i in range(tall)], axis=0
        )
        for half in range(halves)
    ]
    first = core_ref[0:1, :] == 0
    combined = jnp.concatenate(
        [jnp.where(first, own, other), jnp.where(first, other, own)], axis=0
    )
    new = updated(combined, pair_ref[...], gate_ref[...], out_w_ref)
    new_ref[...] = new.astype(F32).reshape(new_ref.shape).astype(BF16)


def on_device(
    alignment,
    pair_features,
    query_matrix,
    key_matrix,
    value_matrix,
    gate_matrix,
    output_matrix,
    bias_weight,
    left_factor_weight,
    right_factor_weight,
    outer_weight,
    outgoing_project,
    outgoing_gate,
    outgoing_output,
    incoming_project,
    incoming_gate,
    incoming_output,
):
    seqs, rows, channels = alignment.shape
    cols, depth = pair_features.shape[1:]
    heads = bias_weight.shape[1]
    factor = left_factor_weight.shape[1]
    places = rows * cols
    full = COLS * cols
    core, x_hi = lax.axis_index("core"), lax.axis_index("xh")

    chunks = kernel_call(
        normed_kernel, [((ROWS, seqs, rows, channels), BF16)], (alignment,), fetched=True
    )[0]
    chunks, later_pair = lax.optimization_barrier((chunks, pair_features))
    bias = kernel_call(
        functools.partial(bias_kernel, rows),
        [((cols, heads * rows), BF16)],
        (later_pair, bias_weight.T),
        fetched=True,
    )[0]
    everyone = exchange(chunks, ROW_X_FIRST)
    bias, query_matrix = from_col(bias, query_matrix)
    queries, gates = kernel_call(
        query_kernel,
        [((seqs, rows, channels), BF16), ((seqs * rows, channels), F32)],
        (alignment, query_matrix, gate_matrix),
    )
    new_alignment, left, right = kernel_call(
        functools.partial(attention_kernel, heads),
        [
            ((seqs, rows, channels), BF16),
            ((seqs, rows * factor), BF16),
            ((ROWS, seqs, rows * factor), BF16),
        ],
        (
            everyone, bias.reshape(full, heads * rows), queries, gates, alignment, key_matrix,
            value_matrix, output_matrix, left_factor_weight.T, right_factor_weight.T,
        ),
        scratch=[((seqs * rows, channels), BF16), ((seqs * rows, 128), F32)],
    )

    size = (rows + cols) * factor
    chunks = kernel_call(
        factor_kernel, [((COLS, seqs, size), BF16)], (left, exchange(right, ROW_X_FIRST))
    )[0]
    factors = exchange(chunks, COL_X_FIRST).reshape(COLS * seqs, size)
    pair_one, left_edge, right_edge = kernel_call(
        outer_kernel,
        [((places, depth), BF16), ((rows, cols, depth), BF16), ((2, SIZES["z"], cols, cols, depth), BF16)],
        (factors, pair_features, outer_weight, outgoing_project),
        scratch=[
            ((cols * factor // 128, rows * factor, 128), F32),
            ((places, depth), F32),
            ((places, depth), F32),
        ],
    )

    chunks = right_edge.reshape((ROWS,) + right_edge.shape[2:])
    tiles = exchange(chunks, ("core", "z")).reshape(right_edge.shape)
    lines = in_order(core, left_edge, flip(left_edge, "core"), axis=1)
    lines = in_order(x_hi, lines, flip(lines, "xh"))
    partial = partial_sums(tiles, lines).reshape(ROWS, rows, cols, depth)
    partial = exchange(partial, ("xl", "y"))
    crossed = cross(pair_one)
    pair_two, chunks, lines = kernel_call(
        middle_kernel,
        [
            ((places, depth), BF16),
            ((SIZES["y"], rows, cols, depth), BF16),
            ((cols, rows, depth), BF16),
        ],
        (partial, crossed, pair_gate(crossed, outgoing_gate), outgoing_output, incoming_project),
        scratch=[((places, depth), F32)],
    )

    own = exchange(chunks, "y")
    lines = in_order(x_hi, lines, flip(lines, "xh"))
    other = flip(own, "core")
    partial = partial_sums(other[None], lines, partial_sums(own[None], lines))
    partial = exchange(partial.reshape(ROWS, 2, cols, cols, depth), ("xl", "z"))
    crossed = cross(pair_two)
    gate = pair_gate(crossed, incoming_gate)
    new_pair = kernel_call(
        last_kernel,
        [((rows, cols, depth), BF16)],
        (jnp.full((8, depth), core), partial, crossed, gate, incoming_output),
        scratch=[((places, depth), F32)],
    )[0]
    return (new_alignment, new_pair)


def solution(mesh):
    fine = jax.sharding.Mesh(mesh.devices.reshape(tuple(SIZES.values())), tuple(SIZES))
    rep = (P(),) * 15
    return jax.shard_map(
        on_device,
        mesh=fine,
        in_specs=(P(COL, ROW, None), P(ROW, COL, None)) + rep,
        out_specs=(P(COL, ROW, None), P(ROW, COL, None)),
        check_vma=False,
    )
```
